256 devices in a mesh: row: 2 (over core), col: 4 (over x), vis: 32 (over z, y).
Axes of the slice: x: 4, y: 4, z: 8, core: 2. Of those that a mesh axis runs over, the one named last changes fastest.
Arguments:
- text_embed: bfloat16 [32, 256, 5120], P('vis', None, 'row'), may hold values from -6 to 6
- image_embed: bfloat16 [32, 64, 5120], P('vis', 'col', 'row'), may hold values from -6 to 6
- slot_source: int32 [32, 256], replicated, may hold values from -1 to 2047, as said below
- segment_ids: int32 [32, 256], P('vis'), may hold values from 0 to 3, never falling along the last dimension, each value on 1 to 128 neighbouring positions
- prefix_lengths: int32 [32, 4], P('vis'), may hold values from 1 to 1024, 2048 in all within a row
- attn_gain: float32 [5120], P('row'), may hold values from 0.1 to 1.9
- qkv_weight: bfloat16 [5120, 3, 5120], P('row', None, 'col'), may hold values from -0.64286954 to 0.64286954
- out_weight: bfloat16 [5120, 5120], P('col', 'row'), may hold values from -0.5 to 0.5
- cache_keys: bfloat16 [32, 4, 1024, 5120], P('vis', None, 'row', 'col'), may hold values from -48 to 48
- cache_values: bfloat16 [32, 4, 1024, 5120], P('vis', None, 'row', 'col'), may hold values from -6 to 6
Outputs:
- hidden: float32 [32, 256, 5120], P('vis', 'col', 'row')
- new_keys: float32 [32, 256, 5120], P('vis', 'row', 'col')
- new_values: float32 [32, 256, 5120], P('vis', 'row', 'col')
- request_rms: float32 [32, 4], P('vis')
The draws below stay inside these ranges and needn't reach their ends.
Inputs may be any that keep to these rules, and one draw needn't show every extreme that they name: `slot_source`: every global image index appears in exactly one slot; all other slots hold -1. The image tokens of one producing group fill at most 4 slots of any one group, and in every draw some group holds exactly 4 image tokens of every producing group.
All inputs are finite; a program needn't handle non-finite values.
Results may differ from the reference program's by a relative error of at most 0.012.
The reference program's roundings to bfloat16 on the way count: a program that leaves them out, or rounds other values in their place, can miss the bound.
Values may be sent and summed in bfloat16 or wider, within the bound.
A program may use at most 192 MiB of HBM per device.

```python
import math
import jax
import jax.numpy as jnp
import numpy as np
from jax import lax

D = 5120
HEADS = 40
HD = 128
TOK_G = 256
REQ_G = 4
PREF = 1024
GROUPS = 32
IMG_G = 64
PAIR_MOST = 4


def draw_slot_source(key, part):
    image_count = GROUPS * IMG_G
    unit_count = GROUPS * PAIR_MOST
    hot_group = jax.random.randint(jax.random.fold_in(key, 1), (), 0, GROUPS).astype(jnp.int32)
    unit_group = jnp.arange(unit_count, dtype=jnp.int32) // PAIR_MOST

    def producer_targets(sub_key):
        shuffle_score = jax.random.permutation(sub_key, unit_count).astype(jnp.int32)
        priority = jnp.where(unit_group == hot_group, 0, unit_count) + shuffle_score
        unit_order = jnp.argsort(priority)
        chosen = unit_group[unit_order[:IMG_G]]
        return chosen[jax.random.permutation(jax.random.fold_in(sub_key, 3), IMG_G)]

    def slot_order(sub_key):
        return jax.random.permutation(sub_key, TOK_G).astype(jnp.int32)
    destinations = jax.vmap(producer_targets)(jax.random.split(jax.random.fold_in(key, 2), GROUPS)).reshape(-1)
    onehot = (destinations[:, None] == jnp.arange(GROUPS, dtype=jnp.int32)[None, :]).astype(jnp.int32)
    arrival_rank = jnp.sum((jnp.cumsum(onehot, axis=0) - onehot) * onehot, axis=1)
    slot_orders = jax.vmap(slot_order)(jax.random.split(jax.random.fold_in(key, 4), GROUPS))
    slot_numbers = slot_orders[destinations, arrival_rank]
    flat_sources = jnp.full((GROUPS * TOK_G,), -1, jnp.int32).at[destinations * TOK_G + slot_numbers].set(jnp.arange(image_count, dtype=jnp.int32))
    return flat_sources.reshape(GROUPS, TOK_G)


def draw_qkv_weight(key, part):
    fan_scale = D ** (-0.5)
    query_part = jnp.clip(jax.random.normal(jax.random.fold_in(key, 11), (D, 1, D), jnp.float32), -6.0, 6.0) * fan_scale
    other_part = jnp.clip(jax.random.normal(jax.random.fold_in(key, 12), (D, 2, D), jnp.float32), -6.0, 6.0) * fan_scale
    return jnp.concatenate([query_part, other_part], axis=1).astype(jnp.bfloat16)


def draw_cache_keys(key, part):
    base_draw = jnp.clip(jax.random.normal(key, (GROUPS, REQ_G, PREF, D), jnp.float32), -6.0, 6.0)
    return base_draw.astype(jnp.bfloat16)


def block_levels(rng, dims, shards, least, high):
    level, own = 1.0, jax.random.fold_in(rng, 6)
    for axis_at, shards_of in shards:
        steps = jnp.exp(jax.random.uniform(jax.random.fold_in(own, axis_at), (shards_of,), jnp.float32, least / len(shards), high / len(shards)))
        level = level * jnp.repeat(steps, dims[axis_at] // shards_of).reshape([-1 if axis == axis_at else 1 for axis in range(len(dims))])
    return level


def split_up(number_of, total, reach, lean):
    portions = [(1 << 20) // math.isqrt(grade ** lean) + 1 for grade in range(2, number_of + 1)]
    spare, given = total - reach - (number_of - 1), [1] * (number_of - 1)
    while spare > 0:
        candidates = [i for i in range(number_of - 1) if given[i] < reach]
        pool, budget = sum([portions[i] for i in candidates]), spare
        for i in candidates:
            addition = min(reach - given[i], max(1, budget * portions[i] // pool), spare)
            given[i] = given[i] + addition
            spare = spare - addition
    return np.array([reach] + given)


def ragged(stream_key, count, total, bound, slope):
    if count == 2:
        one = jax.random.randint(stream_key, (), max(1, total - bound), min(bound, total - 1) + 1)
        return jnp.stack([one, total - one])
    sizes = jnp.asarray(split_up(count, total, bound, slope), jnp.int32)
    couples = (count - 1) // 2
    source_of, sink = sizes[1:1 + 2 * couples:2], sizes[2:2 + 2 * couples:2]
    room = jnp.minimum(source_of - 1, bound - sink)
    passed = jax.random.randint(jax.random.fold_in(stream_key, 1), (couples,), 0, 1 << 20) % (room + 1)
    sizes = sizes.at[1:1 + 2 * couples:2].set(source_of - passed).at[2:2 + 2 * couples:2].set(sink + passed)
    return sizes[jax.random.permutation(jax.random.fold_in(stream_key, 2), count)]


def centred(stream_key, shape, deviation, reach, shards=(), held_as=jnp.bfloat16):
    array = jax.random.normal(stream_key, shape, jnp.float32) * deviation
    if len(shards) > 0:
        array = block_levels(stream_key, shape, shards, -0.22, 0.18) * array
    return jnp.clip(array, min=-reach, max=reach).astype(held_as)


def setup_inputs(seed: int = 0) -> dict:
    keys = jax.random.split(jax.random.key(seed), 11)
    text_embed = centred(keys[0], (GROUPS, TOK_G, D), 1.0, 6.0, ((0, 32), (2, 2)))
    image_embed = centred(keys[1], (GROUPS, IMG_G, D), 1.0, 6.0, ((0, 32), (1, 4), (2, 2)))
    slot_source = draw_slot_source(jax.random.fold_in(keys[10], 71), 0)
    segment_ids = jax.vmap(lambda own: jnp.searchsorted(jnp.cumsum(ragged(own, REQ_G, TOK_G, TOK_G // 2, 2)), jnp.arange(TOK_G), side="right"))(jax.random.split(keys[3], GROUPS)).reshape((GROUPS, TOK_G)).astype(jnp.int32)
    prefix_lengths = jax.vmap(lambda own: ragged(own, REQ_G, REQ_G * PREF // 2, PREF, 2))(jax.random.split(keys[4], GROUPS)).reshape((GROUPS, REQ_G)).astype(jnp.int32)
    attn_gain = jnp.clip(1.0 + 0.18 * jax.random.normal(keys[5], (D,), jnp.float32), 0.1, 1.9)
    qkv_weight = draw_qkv_weight(jax.random.fold_in(keys[10], 71), 0)
    out_weight = centred(keys[7], (D, D), HD ** -0.5, 0.5, ((0, 4), (1, 2)))
    cache_keys = draw_cache_keys(jax.random.fold_in(keys[10], 71), 0)
    cache_values = centred(keys[9], (GROUPS, REQ_G, PREF, D), 1.0, 6.0, ((0, 32), (2, 2), (3, 4)))
    return {"text_embed": text_embed, "image_embed": image_embed, "slot_source": slot_source, "segment_ids": segment_ids, "prefix_lengths": prefix_lengths, "attn_gain": attn_gain, "qkv_weight": qkv_weight, "out_weight": out_weight, "cache_keys": cache_keys, "cache_values": cache_values}


EPSILON = 1e-06

def attend_group(queries, key_rows, value_rows, allowed):

    def one_head(operands):
        head_queries, head_keys, head_values = operands
        scores = jnp.dot(head_queries, head_keys.T, preferred_element_type=jnp.float32) * HD ** (-0.5)
        masked = jnp.where(allowed, scores, -1e+30)
        peak_score = lax.optimization_barrier(jnp.max(masked, axis=1, keepdims=True))
        weights = jnp.where(allowed, jnp.exp(masked - peak_score), 0.0)
        weight_sum = lax.optimization_barrier(jnp.sum(weights, axis=1, keepdims=True))
        summed = jnp.dot(weights.astype(jnp.bfloat16), head_values, preferred_element_type=jnp.float32)
        return summed / weight_sum
    outputs = lax.map(one_head, (queries.transpose(1, 0, 2), key_rows.transpose(1, 0, 2), value_rows.transpose(1, 0, 2)))
    return outputs.transpose(1, 0, 2).reshape(queries.shape[0], -1).astype(jnp.bfloat16)

def reference(text_embed, image_embed, slot_source, segment_ids, prefix_lengths, attn_gain, qkv_weight, out_weight, cache_keys, cache_values):
    flat_images = image_embed.reshape(-1, D)
    hidden_list, key_list, value_list, norm_list = ([], [], [], [])
    request_ids = jnp.arange(REQ_G, dtype=jnp.int32)
    token_ids = jnp.arange(TOK_G, dtype=jnp.int32)
    cache_request = jnp.repeat(request_ids, PREF)
    cache_position = jnp.tile(jnp.arange(PREF, dtype=jnp.int32), REQ_G)
    for group_index in range(GROUPS):
        sources = slot_source[group_index]
        picked_rows = jnp.take(flat_images, jnp.maximum(sources, 0).astype(jnp.int32), axis=0)
        filled = jnp.where((sources >= 0)[:, None], picked_rows, text_embed[group_index])
        wide_rows = filled.astype(jnp.float32)
        square_sums = lax.optimization_barrier(jnp.sum(wide_rows * wide_rows, axis=1))
        inv_rms = lax.rsqrt(square_sums / D + EPSILON)
        scaled = (wide_rows * attn_gain).astype(jnp.bfloat16)
        projected = jnp.dot(scaled, qkv_weight.reshape(D, 3 * D), preferred_element_type=jnp.float32).reshape(TOK_G, 3, D)
        normed = projected * inv_rms[:, None, None]
        rounded = normed.astype(jnp.bfloat16)
        segments = segment_ids[group_index]
        lengths = prefix_lengths[group_index]
        cache_ok = (cache_request[None, :] == segments[:, None]) & (cache_position < lengths[cache_request])[None, :]
        prompt_ok = (segments[None, :] == segments[:, None]) & (token_ids[None, :] <= token_ids[:, None])
        allowed = jnp.concatenate([cache_ok, prompt_ok], axis=1)
        key_rows = jnp.concatenate([cache_keys[group_index].reshape(REQ_G * PREF, D), rounded[:, 1]], axis=0)
        value_rows = jnp.concatenate([cache_values[group_index].reshape(REQ_G * PREF, D), rounded[:, 2]], axis=0)
        attended = attend_group(rounded[:, 0].reshape(TOK_G, HEADS, HD), key_rows.reshape(-1, HEADS, HD), value_rows.reshape(-1, HEADS, HD), allowed)
        update = jnp.dot(attended, out_weight, preferred_element_type=jnp.float32)
        hidden_list.append(wide_rows + update)
        key_list.append(normed[:, 1])
        value_list.append(normed[:, 2])
        onehot = (segments[None, :] == request_ids[:, None]).astype(jnp.float32)
        totals = jnp.dot(onehot, square_sums, precision=lax.Precision.HIGHEST)
        counts = lax.optimization_barrier(jnp.sum(onehot, axis=1))
        norm_list.append(jnp.sqrt(totals / (counts * D)))
    return (jnp.stack(hidden_list), jnp.stack(key_list), jnp.stack(value_list), jnp.stack(norm_list))
```

```python
import functools

import jax
import jax.numpy as jnp
from jax import lax
from jax.experimental import pallas as pl
from jax.experimental.pallas import tpu as pltpu
from jax.sharding import PartitionSpec as P

D = 5120
HD = 128
EPSILON = 1e-06
MASKED = -1e30
SCALE_LOG2E = HD ** (-0.5) * 1.4426950408889634

MESH = pl.DeviceIdType.MESH
F32 = jnp.float32
BF16 = jnp.bfloat16

COLS = 4
ZS = 8
YS = 4
TOK = 256
FEAT = 2560
QUART = 640
WIDTH = 1280
HEADS_HERE = 10
CACHE = 512
REQS = 4
HALF = 128
SHARE = 64
TILE = 512
TILES = FEAT // TILE
Z_ORDER = (1, 7, 2, 6, 3, 5, 4)


def nt_dot(left, right):
    return lax.dot_general(left, right, (((1,), (1,)), ((), ())), preferred_element_type=F32)


def nn_dot(left, right):
    return jnp.dot(left, right, preferred_element_type=F32)


def kernel(
    text_hbm, image_hbm, slots_ref, seg_ref, lens_ref, gain_ref, w_hbm, ow_hbm, ck_hbm, cv_hbm,
    hid_hbm, nk_hbm, nv_hbm, rms_ref,
    w, ow, ck, cv, fill, gath, zsend, compact, scaled,
    sq_own, sq_peer, inv, kv_own, kv_send, kv_recv, q_own, q_send, q_recv, q_bf, kv_bf, kv_out,
    ext, onehot, bias, scores, o_own, o_peer, st_own, st_peer, att,
    upd, hop_a, hop_b, got_a, got_b, out_l, out_r, fin_l, fin_r, hid,
    w_sem, in_sem, out_sem, xy_send, xy_recv, z_send, z_recv, x_send, x_recv,
    pr_send, pr_recv, o_send, o_recv, r_send, r_recv,
):
    row = lax.axis_index("row")
    col = lax.axis_index("col")
    vis = lax.axis_index("vis")
    z = lax.div(vis, YS)
    y = lax.rem(vis, YS)
    other = 1 - row
    right = lax.rem(col + 1, COLS)
    left = lax.rem(col + COLS - 1, COLS)
    across = lax.rem(col + 2, COLS)

    def at(r, c, v):
        return (r, c, v)

    loads_w = []
    for j in (1, 2, 0):
        for part in range(4):
            rows = pl.ds(part * QUART, QUART)
            cp = pltpu.make_async_copy(w_hbm.at[j, rows], w.at[j, rows], w_sem.at[j * 4 + part])
            loads_w.append((j, cp))
    load_text = pltpu.make_async_copy(text_hbm, fill, in_sem.at[0])
    load_k = [pltpu.make_async_copy(ck_hbm.at[s], ck.at[s], in_sem.at[1 + s]) for s in range(REQS)]
    load_v = [pltpu.make_async_copy(cv_hbm.at[s], cv.at[s], in_sem.at[5 + s]) for s in range(REQS)]
    load_ow = [
        pltpu.make_async_copy(ow_hbm.at[pl.ds(p * 320, 320)], ow.at[pl.ds(p * 320, 320)], in_sem.at[9 + p])
        for p in range(4)
    ]
    block = y * COLS + col
    own_rows = pl.ds(pl.multiple_of(block * 16, 16), 16)
    own_cols = pl.ds(pl.multiple_of(col * QUART, 128), QUART)
    load_own = pltpu.make_async_copy(image_hbm.at[:, own_cols], gath.at[own_rows], in_sem.at[13])
    load_own.start()
    load_text.start()

    barrier = pltpu.get_barrier_semaphore()
    for step in range(1, 16):
        to = lax.rem(block + step, 16)
        pl.semaphore_signal(
            barrier, inc=1, device_id=at(row, lax.rem(to, COLS), z * YS + lax.div(to, COLS)), device_id_type=MESH)
    for step in range(1, ZS):
        pl.semaphore_signal(
            barrier, inc=1, device_id=at(row, col, lax.rem(z + step, ZS) * YS + y), device_id_type=MESH)
    pl.semaphore_signal(barrier, inc=1, device_id=at(other, col, vis), device_id_type=MESH)
    for _, cp in loads_w:
        cp.start()

    lane256 = lax.broadcasted_iota(jnp.int32, (128, TOK), 1)
    sub128 = lax.broadcasted_iota(jnp.int32, (128, TOK), 0)
    before = jnp.where(
        lax.broadcasted_iota(jnp.int32, (TOK, TOK), 0) < lax.broadcasted_iota(jnp.int32, (TOK, TOK), 1), 1.0, 0.0
    ).astype(BF16)
    to_rows = jnp.concatenate(
        [jnp.broadcast_to(slots_ref[pl.ds(zz * YS + y, 1), :], (16, TOK)) for zz in range(ZS)], axis=0)
    rank_of = sub128 & 3
    match = (to_rows >> 6) == (z * YS + ((sub128 & 15) >> 2))
    earlier = nn_dot(jnp.where(match, 1.0, 0.0).astype(BF16), before)
    chosen = match & (earlier.astype(jnp.int32) == rank_of)
    token_at = jnp.sum(
        jnp.where(chosen, (to_rows - z * TOK + 1).astype(F32), 0.0), axis=1, keepdims=True).astype(jnp.int32) - 1
    select = jnp.where(token_at == lane256, 1.0, 0.0).astype(BF16)

    here_rows = jnp.broadcast_to(slots_ref[pl.ds(vis, 1), :], (128, TOK))
    here = (here_rows >> 6) == (sub128 >> 2)
    here_before = nn_dot(jnp.where(here, 1.0, 0.0).astype(BF16), before)
    place_f = jnp.where(here & (here_before.astype(jnp.int32) == rank_of), 1.0, 0.0).T
    place = place_f.astype(BF16)
    has_image = jnp.sum(place_f, axis=1, keepdims=True)

    seg_rows = jnp.broadcast_to(seg_ref[...], (128, TOK))
    oh = jnp.where(seg_rows == sub128, 1.0, 0.0).T
    onehot[...] = oh.astype(BF16)
    lane128 = lax.broadcasted_iota(jnp.int32, (TOK, HALF), 1)
    tok128 = lax.broadcasted_iota(jnp.int32, (TOK, HALF), 0)
    seg_col = jnp.sum(oh * lane128.astype(F32), axis=1, keepdims=True).astype(jnp.int32)
    seg_mine = jnp.where(row == 0, seg_ref[:, :HALF], seg_ref[:, HALF:])
    bias[...] = jnp.where(
        (seg_col == seg_mine) & (lane128 + row * HALF <= tok128), 0.0, MASKED)
    for s in range(REQS):
        lane_c = lax.broadcasted_iota(jnp.int32, (CACHE, HD), 1)
        pos = lax.broadcasted_iota(jnp.int32, (CACHE, HD), 0) + row * CACHE
        seen = (lane_c == s) & (pos < lens_ref[0, s])
        ext[s] = jnp.where(seen | (lane_c >= REQS), 0.0, MASKED).astype(BF16)

    pl.semaphore_wait(barrier, 23)
    for step in range(1, 16):
        to = lax.rem(block + step, 16)
        to_col = lax.rem(to, COLS)
        pltpu.make_async_remote_copy(
            src_ref=image_hbm.at[:, pl.ds(pl.multiple_of(to_col * QUART, 128), QUART)],
            dst_ref=gath.at[own_rows],
            send_sem=xy_send.at[step], recv_sem=xy_recv.at[step],
            device_id=at(row, to_col, z * YS + lax.div(to, COLS)), device_id_type=MESH).start()
    for group in (load_k, load_v, load_ow):
        for cp in group:
            cp.start()
    load_own.wait()
    for step in range(1, 16):
        frm = lax.rem(block + 16 - step, 16)
        rows = pl.ds(pl.multiple_of(frm * 16, 16), 16)
        pltpu.make_async_remote_copy(
            src_ref=gath.at[rows], dst_ref=gath.at[rows],
            send_sem=xy_send.at[step], recv_sem=xy_recv.at[step],
            device_id=at(row, col, vis), device_id_type=MESH).wait_recv()

    def block_at(dz, c_src):
        zz = lax.rem(z + dz, ZS)
        return compact.at[pl.ds(pl.multiple_of(zz * 16, 16), 16), pl.ds(pl.multiple_of(c_src * QUART, 128), QUART)]

    zsend[...] = nn_dot(select, gath[...]).astype(BF16)
    for dz in Z_ORDER:
        zz = lax.rem(z + dz, ZS)
        pltpu.make_async_remote_copy(
            src_ref=zsend.at[pl.ds(pl.multiple_of(zz * 16, 16), 16)],
            dst_ref=block_at(0, col),
            send_sem=z_send.at[dz], recv_sem=z_recv.at[ZS - dz],
            device_id=at(row, col, zz * YS + y), device_id_type=MESH).start()

    def x_copy(dz, c_src, to_col, lane):
        return pltpu.make_async_remote_copy(
            src_ref=block_at(dz, c_src), dst_ref=block_at(dz, c_src),
            send_sem=x_send.at[dz, lane], recv_sem=x_recv.at[dz, lane],
            device_id=at(row, to_col, vis), device_id_type=MESH)

    def z_wait(dz):
        pltpu.make_async_remote_copy(
            src_ref=block_at(dz, col), dst_ref=block_at(dz, col),
            send_sem=z_send.at[dz], recv_sem=z_recv.at[dz],
            device_id=at(row, col, vis), device_id_type=MESH).wait_recv()

    order = (0,) + Z_ORDER
    for i, dz in enumerate(order):
        if dz == 0:
            block_own = pltpu.make_async_copy(
                zsend.at[pl.ds(pl.multiple_of(z * 16, 16), 16)], block_at(0, col), in_sem.at[14])
            block_own.start()
            block_own.wait()
        else:
            z_wait(dz)
        x_copy(dz, col, right, 0).start()
        x_copy(dz, col, left, 1).start()
        if i >= 1:
            forward(x_copy, order[i - 1], i - 1, left, right)
    forward(x_copy, order[-1], len(order) - 1, left, right)
    for i, dz in enumerate(order):
        if i % 2 == 0:
            x_copy(dz, right, left, 1).wait_recv()
        else:
            x_copy(dz, left, right, 0).wait_recv()
        x_copy(dz, across, left, 2).wait_recv()

    load_text.wait()
    squares = jnp.zeros((TOK, HD), F32)
    for n in range(TILES):
        cols = slice(n * TILE, (n + 1) * TILE)
        picked = nn_dot(place, compact[:, cols])
        rows_f = jnp.where(has_image > 0.0, picked, fill[:, cols].astype(F32))
        fill[:, cols] = rows_f.astype(BF16)
        scaled[:, cols] = (rows_f * gain_ref[:, cols]).astype(BF16)
        for k in range(TILE // HD):
            piece = rows_f[:, k * HD:(k + 1) * HD]
            squares = squares + piece * piece
    sq_own[...] = jnp.broadcast_to(jnp.sum(squares, axis=1, keepdims=True), (TOK, HD))

    def to_peer(src, dst, k):
        return pltpu.make_async_remote_copy(
            src_ref=src, dst_ref=dst, send_sem=pr_send.at[k], recv_sem=pr_recv.at[k],
            device_id=at(other, col, vis), device_id_type=MESH)

    sq_copy = to_peer(sq_own, sq_peer, 0)
    sq_copy.start()

    peer_copies = {}
    for j in (1, 2, 0):
        for jj, cp in loads_w:
            if jj == j:
                cp.wait()
        if j == 0:
            def q_body(n, carry):
                lanes = pl.ds(pl.multiple_of(n * 256, 256), 256)
                part = nn_dot(scaled[...], w[0, :, lanes])
                q_own[:, lanes] = part
                q_send[:, lanes] = part.astype(BF16)
                return carry
            lax.fori_loop(0, 5, q_body, 0)
            peer_copies[j] = to_peer(q_send, q_recv, 3)
        else:
            def kv_body(n, carry, j=j):
                lanes = pl.ds(pl.multiple_of(n * 256, 256), 256)
                part = nn_dot(scaled[...], w[j, :, lanes])
                kv_own[j - 1, :, lanes] = jnp.where(row == 0, part[:HALF], part[HALF:])
                kv_send[j - 1, :, lanes] = jnp.where(row == 0, part[HALF:], part[:HALF]).astype(BF16)
                return carry
            lax.fori_loop(0, 5, kv_body, 0)
            peer_copies[j] = to_peer(kv_send.at[j - 1], kv_recv.at[j - 1], j)
        peer_copies[j].start()

    sq_copy.wait()
    total_sq = sq_own[...] + sq_peer[...]
    inv[...] = lax.rsqrt(total_sq / D + EPSILON)
    per_request = jnp.sum(oh * total_sq, axis=0, keepdims=True)
    counts = jnp.sum(oh, axis=0, keepdims=True)
    rms_ref[...] = jnp.sqrt(per_request / (counts * D))[:, :REQS]
    inv_mine = inv[pl.ds(pl.multiple_of(row * HALF, HALF), HALF), :]
    outs = []
    for j, dst in ((1, nk_hbm), (2, nv_hbm)):
        peer_copies[j].wait()
        for h in range(HEADS_HERE):
            lanes = slice(h * HD, (h + 1) * HD)
            value = (kv_own[j - 1, :, lanes] + kv_recv[j - 1, :, lanes].astype(F32)) * inv_mine
            kv_out[j - 1, :, lanes] = value
            kv_bf[j - 1, :, lanes] = value.astype(BF16)
        cp = pltpu.make_async_copy(kv_out.at[j - 1], dst, out_sem.at[j])
        cp.start()
        outs.append(cp)
    peer_copies[0].wait()
    for h in range(HEADS_HERE):
        lanes = slice(h * HD, (h + 1) * HD)
        q_bf[:, lanes] = ((q_own[:, lanes] + q_recv[:, lanes].astype(F32)) * inv[...]).astype(BF16)

    for group in (load_k, load_v):
        for cp in group:
            cp.wait()
    st_own[...] = jnp.zeros((TOK, HD), F32)

    def o_copy(h):
        lanes = pl.ds(pl.multiple_of(h * HD, HD), HD)
        return pltpu.make_async_remote_copy(
            src_ref=o_own.at[:, lanes], dst_ref=o_peer.at[:, lanes],
            send_sem=o_send.at[h], recv_sem=o_recv.at[h],
            device_id=at(other, col, vis), device_id_type=MESH)

    def head(h, carry):
        lanes = pl.ds(pl.multiple_of(h * HD, HD), HD)
        q = q_bf[:, lanes]
        q_ext = jnp.concatenate([q, onehot[...]], axis=1)
        new = nt_dot(q, kv_bf[0, :, lanes]) + bias[...]
        scores[:, REQS * CACHE:] = new
        peak = new
        for s in range(REQS):
            part = nt_dot(q_ext, jnp.concatenate([ck[s, :, lanes], ext[s]], axis=1))
            scores[:, s * CACHE:(s + 1) * CACHE] = part
            for k in range(CACHE // HD):
                peak = jnp.maximum(peak, part[:, k * HD:(k + 1) * HD])
        top = jnp.max(peak, axis=1, keepdims=True) * SCALE_LOG2E
        ones = jnp.ones((CACHE, HD), BF16)
        weights = jnp.exp2(scores[:, REQS * CACHE:] * SCALE_LOG2E - top).astype(BF16)
        acc = nn_dot(weights, jnp.concatenate([kv_bf[1, :, lanes], ones[:HALF]], axis=1))
        for s in range(REQS):
            weights = jnp.exp2(scores[:, s * CACHE:(s + 1) * CACHE] * SCALE_LOG2E - top).astype(BF16)
            acc = acc + nn_dot(weights, jnp.concatenate([cv[s, :, lanes], ones], axis=1))
        total = acc[:, HD:]
        o_own[:, lanes] = (acc[:, :HD] / total).astype(BF16)
        st_own[...] = jnp.where(lane128 == h, top + jnp.log2(total), st_own[...])
        o_copy(h).start()
        return carry

    lax.fori_loop(0, HEADS_HERE, head, 0)
    st_copy = to_peer(st_own, st_peer, 4)
    st_copy.start()
    st_copy.wait()
    lead = st_own[...] - st_peer[...]
    mine = 1.0 / (1.0 + jnp.exp2(-lead))
    theirs = 1.0 / (1.0 + jnp.exp2(lead))
    for h in range(HEADS_HERE):
        lanes = slice(h * HD, (h + 1) * HD)
        o_copy(h).wait()
        att[:, lanes] = (
            o_own[:, lanes].astype(F32) * mine[:, h:h + 1] + o_peer[:, lanes].astype(F32) * theirs[:, h:h + 1]
        ).astype(BF16)

    for cp in load_ow:
        cp.wait()

    def share(c):
        return pl.ds(pl.multiple_of(c * SHARE, SHARE), SHARE)

    def ring(src, dst, k, lane, to_col):
        return pltpu.make_async_remote_copy(
            src_ref=src, dst_ref=dst, send_sem=r_send.at[k, lane], recv_sem=r_recv.at[k, lane],
            device_id=at(row, to_col, vis), device_id_type=MESH)

    def hop(n):
        return (
            ring(hop_a.at[n], got_a.at[n], n, 0, right),
            ring(hop_b.at[n], got_b.at[n], n, 1, left),
        )

    def last(n):
        return (
            ring(out_r.at[n], fin_l.at[n], n, 2, right),
            ring(out_l.at[n], fin_r.at[n], n, 3, left),
        )

    half = TILE // 2

    def second(n):
        one, two = hop(n)
        cols = pl.ds(n * TILE, TILE)
        one.wait_recv()
        two.wait_recv()
        to_right = upd[share(right), cols]
        out_r[n] = jnp.concatenate(
            [to_right[:, :half] + got_a[n].astype(F32), to_right[:, half:]], axis=1).astype(BF16)
        to_left = upd[share(left), cols]
        out_l[n] = jnp.concatenate(
            [to_left[:, :half], to_left[:, half:] + got_b[n].astype(F32)], axis=1).astype(BF16)
        for cp in last(n):
            cp.start()

    for n in range(TILES):
        cols = pl.ds(n * TILE, TILE)
        upd[:, cols] = nn_dot(att[...], ow[:, cols])
        far = upd[share(across), cols]
        hop_a[n] = far[:, :half].astype(BF16)
        hop_b[n] = far[:, half:].astype(BF16)
        for cp in hop(n):
            cp.start()
        if n >= 1:
            second(n - 1)
    second(TILES - 1)
    for n in range(TILES):
        cols = pl.ds(n * TILE, TILE)
        for cp in last(n):
            cp.wait_recv()
        hid[:, cols] = (
            fill[share(col), cols].astype(F32) + upd[share(col), cols]
            + (fin_l[n].astype(F32) + fin_r[n].astype(F32)))
        cp = pltpu.make_async_copy(hid.at[:, cols], hid_hbm.at[:, cols], out_sem.at[3 + n])
        cp.start()
        outs.append(cp)

    for step in range(1, 16):
        pltpu.make_async_remote_copy(
            src_ref=image_hbm.at[:, own_cols], dst_ref=gath.at[own_rows],
            send_sem=xy_send.at[step], recv_sem=xy_recv.at[step],
            device_id=at(other, col, vis), device_id_type=MESH).wait_send()
    for dz in Z_ORDER:
        pltpu.make_async_remote_copy(
            src_ref=zsend.at[pl.ds(0, 16)], dst_ref=block_at(0, col),
            send_sem=z_send.at[dz], recv_sem=z_recv.at[dz],
            device_id=at(other, col, vis), device_id_type=MESH).wait_send()
    for dz in order:
        for lane in range(3):
            x_copy(dz, col, right, lane).wait_send()
    for n in range(TILES):
        for cp in hop(n) + last(n):
            cp.wait_send()
    for cp in outs:
        cp.wait()


def forward(x_copy, dz, i, left, right):
    if i % 2 == 0:
        x_copy(dz, left, right, 0).wait_recv()
        x_copy(dz, left, right, 2).start()
    else:
        x_copy(dz, right, left, 1).wait_recv()
        x_copy(dz, right, left, 2).start()


def per_device(
    text_embed, image_embed, slot_source, segment_ids, prefix_lengths,
    attn_gain, qkv_weight, out_weight, cache_keys, cache_values,
):
    hbm = pl.BlockSpec(memory_space=pl.ANY)
    vmem = pl.BlockSpec(memory_space=pltpu.VMEM)
    smem = pl.BlockSpec(memory_space=pltpu.SMEM)

    def v(shape, dtype):
        return pltpu.VMEM(shape, dtype)

    dma = pltpu.SemaphoreType.DMA
    hidden, keys, values, rms = pl.pallas_call(
        kernel,
        out_shape=(
            jax.ShapeDtypeStruct((SHARE, FEAT), F32),
            jax.ShapeDtypeStruct((HALF, WIDTH), F32),
            jax.ShapeDtypeStruct((HALF, WIDTH), F32),
            jax.ShapeDtypeStruct((1, REQS), F32),
        ),
        in_specs=[hbm, hbm, vmem, vmem, smem, vmem, hbm, hbm, hbm, hbm],
        out_specs=(hbm, hbm, hbm, vmem),
        scratch_shapes=[
            v((3, FEAT, WIDTH), BF16), v((WIDTH, FEAT), BF16),
            v((REQS, CACHE, WIDTH), BF16), v((REQS, CACHE, WIDTH), BF16),
            v((TOK, FEAT), BF16), v((TOK, QUART), BF16), v((HALF, QUART), BF16), v((HALF, FEAT), BF16),
            v((TOK, FEAT), BF16),
            v((TOK, HD), F32), v((TOK, HD), F32), v((TOK, HD), F32),
            v((2, HALF, WIDTH), F32), v((2, HALF, WIDTH), BF16), v((2, HALF, WIDTH), BF16),
            v((TOK, WIDTH), F32), v((TOK, WIDTH), BF16), v((TOK, WIDTH), BF16), v((TOK, WIDTH), BF16),
            v((2, HALF, WIDTH), BF16), v((2, HALF, WIDTH), F32),
            v((REQS, CACHE, HD), BF16), v((TOK, HD), BF16), v((TOK, HALF), F32),
            v((TOK, REQS * CACHE + HALF), F32),
            v((TOK, WIDTH), BF16), v((TOK, WIDTH), BF16), v((TOK, HD), F32), v((TOK, HD), F32),
            v((TOK, WIDTH), BF16),
            v((TOK, FEAT), F32),
            v((TILES, SHARE, TILE // 2), BF16), v((TILES, SHARE, TILE // 2), BF16),
            v((TILES, SHARE, TILE // 2), BF16), v((TILES, SHARE, TILE // 2), BF16),
            v((TILES, SHARE, TILE), BF16), v((TILES, SHARE, TILE), BF16),
            v((TILES, SHARE, TILE), BF16), v((TILES, SHARE, TILE), BF16),
            v((SHARE, FEAT), F32),
            dma((12,)), dma((15,)), dma((8,)), dma((16,)), dma((16,)), dma((8,)), dma((8,)),
            dma((8, 3)), dma((8, 3)), dma((5,)), dma((5,)), dma((HEADS_HERE,)), dma((HEADS_HERE,)),
            dma((TILES, 4)), dma((TILES, 4)),
        ],
        compiler_params=pltpu.CompilerParams(
            collective_id=0, has_side_effects=True, vmem_limit_bytes=60 * 1024 * 1024),
    )(
        text_embed[0], image_embed[0], slot_source, segment_ids, prefix_lengths,
        attn_gain.reshape(1, -1), qkv_weight.transpose(1, 0, 2), out_weight, cache_keys[0], cache_values[0],
    )
    return hidden[None], keys[None], values[None], rms


def solution(mesh):
    return jax.shard_map(
        per_device,
        mesh=mesh,
        in_specs=(
            P("vis", None, "row"),
            P("vis", "col", "row"),
            P(),
            P("vis", None),
            P("vis", None),
            P("row"),
            P("row", None, "col"),
            P("col", "row"),
            P("vis", None, "row", "col"),
            P("vis", None, "row", "col"),
        ),
        out_specs=(
            P("vis", "col", "row"),
            P("vis", "row", "col"),
            P("vis", "row", "col"),
            P("vis", None),
        ),
        check_vma=False,
    )
```

```python
import functools

import jax
import jax.numpy as jnp
from jax import lax
from jax.experimental import pallas as pl
from jax.experimental.pallas import tpu as pltpu
from jax.sharding import PartitionSpec as P

D = 5120
HD = 128
EPSILON = 1e-06
MASKED = -1e30
SCALE_LOG2E = HD ** (-0.5) * 1.4426950408889634

MESH = pl.DeviceIdType.MESH
F32 = jnp.float32
BF16 = jnp.bfloat16

COLS = 4
ZS = 8
YS = 4
TOK = 256
FEAT = 2560
QUART = 640
WIDTH = 1280
HEADS_HERE = 10
CACHE = 512
REQS = 4
HALF = 128
SHARE = 64
TILE = 512
TILES = FEAT // TILE
Z_ORDER = (1, 7, 2, 6, 3, 5, 4)


def nt_dot(left, right):
    return lax.dot_general(left, right, (((1,), (1,)), ((), ())), preferred_element_type=F32)


def nn_dot(left, right):
    return jnp.dot(left, right, preferred_element_type=F32)


def kernel(
    text_hbm, image_hbm, slots_ref, seg_ref, lens_ref, gain_ref, w_hbm, ow_hbm, ck_hbm, cv_hbm,
    hid_hbm, nk_hbm, nv_hbm, rms_ref,
    w, ow, ck, cv, fill, gath, zsend, compact, scaled, gain, acc,
    sq_own, sq_peer, inv, kv_own, kv_send, kv_recv, q_send, q_recv, q_bf, kv_bf,
    ext, onehot, bias, scores, weights, o_own, o_peer, st_own, st_peer, att,
    hop_a, hop_b, got_a, got_b, out_l, out_r, fin_l, fin_r, hid,
    w_sem, in_sem, out_sem, xy_send, xy_recv, z_send, z_recv, x_send, x_recv,
    pr_send, pr_recv, o_send, o_recv, r_send, r_recv,
):
    row = lax.axis_index("row")
    col = lax.axis_index("col")
    vis = lax.axis_index("vis")
    z = lax.div(vis, YS)
    y = lax.rem(vis, YS)
    other = 1 - row
    right = lax.rem(col + 1, COLS)
    left = lax.rem(col + COLS - 1, COLS)
    across = lax.rem(col + 2, COLS)

    def at(r, c, v):
        return (r, c, v)

    block = y * COLS + col
    barrier = pltpu.get_barrier_semaphore()
    for step in range(1, 16):
        to = lax.rem(block + step, 16)
        pl.semaphore_signal(
            barrier, inc=1, device_id=at(row, lax.rem(to, COLS), z * YS + lax.div(to, COLS)), device_id_type=MESH)
    for step in range(1, ZS):
        pl.semaphore_signal(
            barrier, inc=1, device_id=at(row, col, lax.rem(z + step, ZS) * YS + y), device_id_type=MESH)
    pl.semaphore_signal(barrier, inc=1, device_id=at(other, col, vis), device_id_type=MESH)
    loads_w = []
    for j in (1, 2, 0):
        for part in range(4):
            rows = pl.ds(part * QUART, QUART)
            cp = pltpu.make_async_copy(w_hbm.at[j, rows], w.at[j, rows], w_sem.at[j * 4 + part])
            loads_w.append((j, cp))
    load_text = pltpu.make_async_copy(text_hbm, fill, in_sem.at[0])
    load_k = [pltpu.make_async_copy(ck_hbm.at[s], ck.at[s], in_sem.at[1 + s]) for s in range(REQS)]
    load_v = [pltpu.make_async_copy(cv_hbm.at[s], cv.at[s], in_sem.at[5 + s]) for s in range(REQS)]
    load_ow = [
        pltpu.make_async_copy(ow_hbm.at[pl.ds(p * 320, 320)], ow.at[pl.ds(p * 320, 320)], in_sem.at[9 + p])
        for p in range(4)
    ]
    own_rows = pl.ds(pl.multiple_of(block * 16, 16), 16)
    own_cols = pl.ds(pl.multiple_of(col * QUART, 128), QUART)
    load_own = pltpu.make_async_copy(image_hbm.at[:, own_cols], gath.at[own_rows], in_sem.at[13])
    load_own.start()
    load_text.start()

    pl.semaphore_wait(barrier, 23)
    for step in range(1, 16):
        to = lax.rem(block + step, 16)
        to_col = lax.rem(to, COLS)
        pltpu.make_async_remote_copy(
            src_ref=image_hbm.at[:, pl.ds(pl.multiple_of(to_col * QUART, 128), QUART)],
            dst_ref=gath.at[own_rows],
            send_sem=xy_send.at[step], recv_sem=xy_recv.at[step],
            device_id=at(row, to_col, z * YS + lax.div(to, COLS)), device_id_type=MESH).start()
    for _, cp in loads_w:
        cp.start()

    load_text.wait()
    for k in range(FEAT // HD):
        gain[:, k * HD:(k + 1) * HD] = jnp.broadcast_to(gain_ref[pl.ds(k * HD, HD)].reshape(1, HD), (8, HD))

    lane256 = lax.broadcasted_iota(jnp.int32, (128, TOK), 1)
    sub128 = lax.broadcasted_iota(jnp.int32, (128, TOK), 0)
    before = jnp.where(
        lax.broadcasted_iota(jnp.int32, (TOK, TOK), 0) < lax.broadcasted_iota(jnp.int32, (TOK, TOK), 1), 1.0, 0.0
    ).astype(BF16)
    to_rows = jnp.concatenate(
        [jnp.broadcast_to(slots_ref[pl.ds(zz * YS + y, 1), :], (16, TOK)) for zz in range(ZS)], axis=0)
    rank_of = sub128 & 3
    match = (to_rows >> 6) == (z * YS + ((sub128 & 15) >> 2))
    earlier = nn_dot(jnp.where(match, 1.0, 0.0).astype(BF16), before)
    chosen = match & (earlier.astype(jnp.int32) == rank_of)
    token_at = jnp.sum(
        jnp.where(chosen, (to_rows - z * TOK + 1).astype(F32), 0.0), axis=1, keepdims=True).astype(jnp.int32) - 1
    select = jnp.where(token_at == lane256, 1.0, 0.0).astype(BF16)

    here_rows = jnp.broadcast_to(slots_ref[pl.ds(vis, 1), :], (128, TOK))
    here = (here_rows >> 6) == (sub128 >> 2)
    here_before = nn_dot(jnp.where(here, 1.0, 0.0).astype(BF16), before)
    place_f = jnp.where(here & (here_before.astype(jnp.int32) == rank_of), 1.0, 0.0).T
    place = place_f.astype(BF16)
    has_image = jnp.sum(place_f, axis=1, keepdims=True)

    seg_rows = jnp.broadcast_to(seg_ref[...], (128, TOK))
    oh = jnp.where(seg_rows == sub128, 1.0, 0.0).T
    onehot[...] = oh.astype(BF16)
    lane128 = lax.broadcasted_iota(jnp.int32, (TOK, HALF), 1)
    tok128 = lax.broadcasted_iota(jnp.int32, (TOK, HALF), 0)
    seg_col = jnp.sum(oh * lane128.astype(F32), axis=1, keepdims=True).astype(jnp.int32)
    seg_mine = jnp.where(row == 0, seg_ref[:, :HALF], seg_ref[:, HALF:])
    bias[...] = jnp.where(
        (seg_col == seg_mine) & (lane128 + row * HALF <= tok128), 0.0, MASKED)
    for s in range(REQS):
        lane_c = lax.broadcasted_iota(jnp.int32, (CACHE, HD), 1)
        pos = lax.broadcasted_iota(jnp.int32, (CACHE, HD), 0) + row * CACHE
        seen = (lane_c == s) & (pos < lens_ref[0, s])
        ext[s] = jnp.where(seen | (lane_c >= REQS), 0.0, MASKED).astype(BF16)

    load_own.wait()
    for step in range(1, 16):
        frm = lax.rem(block + 16 - step, 16)
        rows = pl.ds(pl.multiple_of(frm * 16, 16), 16)
        pltpu.make_async_remote_copy(
            src_ref=gath.at[rows], dst_ref=gath.at[rows],
            send_sem=xy_send.at[step], recv_sem=xy_recv.at[step],
            device_id=at(row, col, vis), device_id_type=MESH).wait_recv()

    def block_at(dz, c_src):
        zz = lax.rem(z + dz, ZS)
        return compact.at[pl.ds(pl.multiple_of(zz * 16, 16), 16), pl.ds(pl.multiple_of(c_src * QUART, 128), QUART)]

    picked_rows = nn_dot(select, gath[...]).astype(BF16)
    zsend[...] = picked_rows
    for dz in Z_ORDER:
        zz = lax.rem(z + dz, ZS)
        pltpu.make_async_remote_copy(
            src_ref=zsend.at[pl.ds(pl.multiple_of(zz * 16, 16), 16)],
            dst_ref=block_at(0, col),
            send_sem=z_send.at[dz], recv_sem=z_recv.at[ZS - dz],
            device_id=at(row, col, zz * YS + y), device_id_type=MESH).start()
    block_own = pltpu.make_async_copy(
        zsend.at[pl.ds(pl.multiple_of(z * 16, 16), 16)], block_at(0, col), in_sem.at[14])
    block_own.start()
    for group in (load_k, load_v, load_ow):
        for cp in group:
            cp.start()

    def quarter(c_src):
        return pl.ds(pl.multiple_of(c_src * QUART, 128), QUART)

    def x_copy(c_src, to_col, lane):
        part = compact.at[:, quarter(c_src)]
        return pltpu.make_async_remote_copy(
            src_ref=part, dst_ref=part, send_sem=x_send.at[lane], recv_sem=x_recv.at[lane],
            device_id=at(row, to_col, vis), device_id_type=MESH)

    block_own.wait()
    for dz in Z_ORDER:
        pltpu.make_async_remote_copy(
            src_ref=block_at(dz, col), dst_ref=block_at(dz, col),
            send_sem=z_send.at[dz], recv_sem=z_recv.at[dz],
            device_id=at(row, col, vis), device_id_type=MESH).wait_recv()
    x_sends = [x_copy(col, right, 0), x_copy(col, left, 1), x_copy(col, across, 2)]
    for cp in x_sends[:2]:
        cp.start()

    def to_peer(src, dst, k):
        return pltpu.make_async_remote_copy(
            src_ref=src, dst_ref=dst, send_sem=pr_send.at[k], recv_sem=pr_recv.at[k],
            device_id=at(other, col, vis), device_id_type=MESH)

    def fill_quarter(c_src, squares):
        cols = quarter(c_src)
        rows_f = jnp.where(has_image > 0.0, nn_dot(place, compact[:, cols]), fill[:, cols].astype(F32))
        fill[:, cols] = rows_f.astype(BF16)
        scaled[:, cols] = (rows_f * gain[0:1, cols]).astype(BF16)
        for k in range(QUART // HD):
            piece = rows_f[:, k * HD:(k + 1) * HD]
            squares = squares + piece * piece
        return squares

    def product(c_src, j):
        return nn_dot(scaled[:, quarter(c_src)], w[j, quarter(c_src), :])

    def out_cols(j):
        return slice(j * WIDTH, (j + 1) * WIDTH)

    squares = fill_quarter(col, jnp.zeros((TOK, HD), F32))
    for jj, cp in loads_w:
        cp.wait()
    for j in range(3):
        acc[:, out_cols(j)] = product(col, j)
    for cp in x_sends[:2]:
        cp.wait_send()
    x_sends[2].start()
    for c_src, lane in ((left, 0), (right, 1)):
        x_copy(c_src, right, lane).wait_recv()
        squares = fill_quarter(c_src, squares)
    for j in range(3):
        acc[:, out_cols(j)] += product(left, j)
        acc[:, out_cols(j)] += product(right, j)
    x_copy(across, right, 2).wait_recv()
    squares = fill_quarter(across, squares)
    sq_own[...] = jnp.broadcast_to(jnp.sum(squares, axis=1, keepdims=True), (TOK, HD))
    sq_copy = to_peer(sq_own, sq_peer, 0)
    sq_copy.start()
    peer_copies = {0: to_peer(q_send, q_recv, 3)}
    acc[:, out_cols(0)] += product(across, 0)
    q_send[...] = acc[:, out_cols(0)].astype(BF16)
    peer_copies[0].start()
    my_rows = pl.ds(pl.multiple_of(row * HALF, HALF), HALF)
    its_rows = pl.ds(pl.multiple_of(other * HALF, HALF), HALF)
    for j in (1, 2):
        acc[:, out_cols(j)] += product(across, j)
        kv_send[j - 1] = acc[its_rows, out_cols(j)].astype(BF16)
        peer_copies[j] = to_peer(kv_send.at[j - 1], kv_recv.at[j - 1], j)
        peer_copies[j].start()

    sq_copy.wait()
    total_sq = sq_own[...] + sq_peer[...]
    inv[...] = lax.rsqrt(total_sq / D + EPSILON)
    per_request = jnp.sum(oh * total_sq, axis=0, keepdims=True)
    counts = jnp.sum(oh, axis=0, keepdims=True)
    rms_ref[...] = jnp.sqrt(per_request / (counts * D))[:, :REQS]
    inv_mine = inv[my_rows, :]
    outs = []
    peer_copies[0].wait()
    for h in range(HEADS_HERE):
        lanes = slice(h * HD, (h + 1) * HD)
        q_bf[:, lanes] = ((acc[:, lanes] + q_recv[:, lanes].astype(F32)) * inv[...]).astype(BF16)

    def finish_new(j, dst):
        peer_copies[j].wait()
        for h in range(HEADS_HERE):
            lanes = slice(h * HD, (h + 1) * HD)
            value = (acc[my_rows, j * WIDTH + h * HD:j * WIDTH + (h + 1) * HD] + kv_recv[j - 1, :, lanes].astype(F32)) * inv_mine
            kv_own[j - 1, :, lanes] = value
            kv_bf[j - 1, :, lanes] = value.astype(BF16)
        cp = pltpu.make_async_copy(kv_own.at[j - 1], dst, out_sem.at[j])
        cp.start()
        outs.append(cp)

    finish_new(1, nk_hbm)

    for group in (load_k, load_v):
        for cp in group:
            cp.wait()
    st_own[...] = jnp.zeros((TOK, HD), F32)

    def o_copy(h):
        lanes = pl.ds(pl.multiple_of(h * HD, HD), HD)
        return pltpu.make_async_remote_copy(
            src_ref=o_own.at[:, lanes], dst_ref=o_peer.at[:, lanes],
            send_sem=o_send.at[h], recv_sem=o_recv.at[h],
            device_id=at(other, col, vis), device_id_type=MESH)

    def weigh(h):
        lanes = pl.ds(pl.multiple_of(h * HD, HD), HD)
        q = q_bf[:, lanes]
        q_ext = jnp.concatenate([q, onehot[...]], axis=1)
        peak = nt_dot(q, kv_bf[0, :, lanes]) + bias[...]
        scores[:, REQS * CACHE:] = peak
        for s in range(REQS):
            part = nt_dot(q_ext, jnp.concatenate([ck[s, :, lanes], ext[s]], axis=1))
            scores[:, s * CACHE:(s + 1) * CACHE] = part
            for k in range(CACHE // HD):
                peak = jnp.maximum(peak, part[:, k * HD:(k + 1) * HD])
        top = jnp.max(peak, axis=1, keepdims=True) * SCALE_LOG2E
        weights[...] = jnp.exp2(scores[...] * SCALE_LOG2E - top).astype(BF16)
        return top

    def gather_values(h, top):
        lanes = pl.ds(pl.multiple_of(h * HD, HD), HD)
        ones = jnp.ones((CACHE, HD), BF16)
        total_acc = nn_dot(
            weights[:, REQS * CACHE:], jnp.concatenate([kv_bf[1, :, lanes], ones[:HALF]], axis=1))
        for s in range(REQS):
            total_acc = total_acc + nn_dot(
                weights[:, s * CACHE:(s + 1) * CACHE], jnp.concatenate([cv[s, :, lanes], ones], axis=1))
        total = total_acc[:, HD:]
        o_own[:, lanes] = (total_acc[:, :HD] / total).astype(BF16)
        st_own[...] = jnp.where(lane128 == h, top + jnp.log2(total), st_own[...])

    top = weigh(0)
    finish_new(2, nv_hbm)

    def head(h, top):
        gather_values(h, top)
        top = weigh(h + 1)
        o_copy(h).start()
        return top

    top = lax.fori_loop(0, HEADS_HERE - 1, head, top)
    gather_values(HEADS_HERE - 1, top)
    o_copy(HEADS_HERE - 1).start()
    st_copy = to_peer(st_own, st_peer, 4)
    st_copy.start()
    st_copy.wait()
    lead = st_own[...] - st_peer[...]
    mine = 1.0 / (1.0 + jnp.exp2(-lead))
    theirs = 1.0 / (1.0 + jnp.exp2(lead))
    for h in range(HEADS_HERE):
        lanes = slice(h * HD, (h + 1) * HD)
        o_copy(h).wait()
        att[:, lanes] = (
            o_own[:, lanes].astype(F32) * mine[:, h:h + 1] + o_peer[:, lanes].astype(F32) * theirs[:, h:h + 1]
        ).astype(BF16)

    for cp in load_ow:
        cp.wait()

    def share(c):
        return pl.ds(pl.multiple_of(c * SHARE, SHARE), SHARE)

    def ring(src, dst, k, lane, to_col):
        return pltpu.make_async_remote_copy(
            src_ref=src, dst_ref=dst, send_sem=r_send.at[k, lane], recv_sem=r_recv.at[k, lane],
            device_id=at(row, to_col, vis), device_id_type=MESH)

    def hop(n):
        return (
            ring(hop_a.at[n], got_a.at[n], n, 0, right),
            ring(hop_b.at[n], got_b.at[n], n, 1, left),
        )

    def last(n):
        return (
            ring(out_r.at[n], fin_l.at[n], n, 2, right),
            ring(out_l.at[n], fin_r.at[n], n, 3, left),
        )

    half = TILE // 2

    def second(n):
        one, two = hop(n)
        cols = pl.ds(n * TILE, TILE)
        one.wait_recv()
        two.wait_recv()
        to_right = acc[share(right), cols]
        out_r[n] = jnp.concatenate(
            [to_right[:, :half] + got_a[n].astype(F32), to_right[:, half:]], axis=1).astype(BF16)
        to_left = acc[share(left), cols]
        out_l[n] = jnp.concatenate(
            [to_left[:, :half], to_left[:, half:] + got_b[n].astype(F32)], axis=1).astype(BF16)
        for cp in last(n):
            cp.start()

    for n in range(TILES):
        cols = pl.ds(n * TILE, TILE)
        acc[:, cols] = nn_dot(att[...], ow[:, cols])
        far = acc[share(across), cols]
        hop_a[n] = far[:, :half].astype(BF16)
        hop_b[n] = far[:, half:].astype(BF16)
        for cp in hop(n):
            cp.start()
        if n >= 1:
            second(n - 1)
    second(TILES - 1)
    for n in range(TILES):
        cols = pl.ds(n * TILE, TILE)
        for cp in last(n):
            cp.wait_recv()
        hid[:, cols] = (
            fill[share(col), cols].astype(F32) + acc[share(col), cols]
            + (fin_l[n].astype(F32) + fin_r[n].astype(F32)))
        cp = pltpu.make_async_copy(hid.at[:, cols], hid_hbm.at[:, cols], out_sem.at[3 + n])
        cp.start()
        outs.append(cp)

    for step in range(1, 16):
        pltpu.make_async_remote_copy(
            src_ref=image_hbm.at[:, own_cols], dst_ref=gath.at[own_rows],
            send_sem=xy_send.at[step], recv_sem=xy_recv.at[step],
            device_id=at(other, col, vis), device_id_type=MESH).wait_send()
    for dz in Z_ORDER:
        pltpu.make_async_remote_copy(
            src_ref=zsend.at[pl.ds(0, 16)], dst_ref=block_at(0, col),
            send_sem=z_send.at[dz], recv_sem=z_recv.at[dz],
            device_id=at(other, col, vis), device_id_type=MESH).wait_send()
    x_sends[2].wait_send()
    for n in range(TILES):
        for cp in hop(n) + last(n):
            cp.wait_send()
    for cp in outs:
        cp.wait()


def hand_over(*refs):
    ins, outs, held, sems = refs[:4], refs[4:8], refs[8:11], refs[11]
    chunks = []
    for i in range(3):
        rows = ins[i].shape[0] // 2
        for k in range(2):
            part = pl.ds(k * rows, rows)
            chunks.append((
                pltpu.make_async_copy(ins[i].at[part], held[i].at[part], sems.at[0, 2 * i + k]),
                pltpu.make_async_copy(held[i].at[part], outs[i].at[part], sems.at[1, 2 * i + k]),
            ))
    for one, _ in chunks:
        one.start()
    outs[3][...] = ins[3][...]
    for one, two in chunks:
        one.wait()
        two.start()
    for _, two in chunks:
        two.wait()


def per_device(
    text_embed, image_embed, slot_source, segment_ids, prefix_lengths,
    attn_gain, qkv_weight, out_weight, cache_keys, cache_values,
):
    hbm = pl.BlockSpec(memory_space=pl.ANY)
    vmem = pl.BlockSpec(memory_space=pltpu.VMEM)
    smem = pl.BlockSpec(memory_space=pltpu.SMEM)

    def v(shape, dtype):
        return pltpu.VMEM(shape, dtype)

    dma = pltpu.SemaphoreType.DMA
    results = (
        jax.ShapeDtypeStruct((SHARE, FEAT), F32),
        jax.ShapeDtypeStruct((HALF, WIDTH), F32),
        jax.ShapeDtypeStruct((HALF, WIDTH), F32),
        jax.ShapeDtypeStruct((1, REQS), F32),
    )
    made = pl.pallas_call(
        kernel,
        out_shape=results,
        in_specs=[hbm, hbm, vmem, vmem, smem, vmem, hbm, hbm, hbm, hbm],
        out_specs=(hbm, hbm, hbm, vmem),
        scratch_shapes=[
            v((3, FEAT, WIDTH), BF16), v((WIDTH, FEAT), BF16),
            v((REQS, CACHE, WIDTH), BF16), v((REQS, CACHE, WIDTH), BF16),
            v((TOK, FEAT), BF16), v((TOK, QUART), BF16), v((HALF, QUART), BF16), v((HALF, FEAT), BF16),
            v((TOK, FEAT), BF16), v((8, FEAT), F32), v((TOK, 3 * WIDTH), F32),
            v((TOK, HD), F32), v((TOK, HD), F32), v((TOK, HD), F32),
            v((2, HALF, WIDTH), F32), v((2, HALF, WIDTH), BF16), v((2, HALF, WIDTH), BF16),
            v((TOK, WIDTH), BF16), v((TOK, WIDTH), BF16), v((TOK, WIDTH), BF16),
            v((2, HALF, WIDTH), BF16),
            v((REQS, CACHE, HD), BF16), v((TOK, HD), BF16), v((TOK, HALF), F32),
            v((TOK, REQS * CACHE + HALF), F32), v((TOK, REQS * CACHE + HALF), BF16),
            v((TOK, WIDTH), BF16), v((TOK, WIDTH), BF16), v((TOK, HD), F32), v((TOK, HD), F32),
            v((TOK, WIDTH), BF16),
            v((TILES, SHARE, TILE // 2), BF16), v((TILES, SHARE, TILE // 2), BF16),
            v((TILES, SHARE, TILE // 2), BF16), v((TILES, SHARE, TILE // 2), BF16),
            v((TILES, SHARE, TILE), BF16), v((TILES, SHARE, TILE), BF16),
            v((TILES, SHARE, TILE), BF16), v((TILES, SHARE, TILE), BF16),
            v((SHARE, FEAT), F32),
            dma((12,)), dma((15,)), dma((8,)), dma((16,)), dma((16,)), dma((8,)), dma((8,)),
            dma((3,)), dma((3,)), dma((5,)), dma((5,)), dma((HEADS_HERE,)), dma((HEADS_HERE,)),
            dma((TILES, 4)), dma((TILES, 4)),
        ],
        compiler_params=pltpu.CompilerParams(
            collective_id=0, has_side_effects=True, vmem_limit_bytes=60 * 1024 * 1024),
    )(
        text_embed[0], image_embed[0], slot_source, segment_ids, prefix_lengths,
        attn_gain, qkv_weight.transpose(1, 0, 2), out_weight, cache_keys[0], cache_values[0],
    )
    hidden, keys, values, rms = pl.pallas_call(
        hand_over,
        out_shape=results,
        in_specs=[hbm, hbm, hbm, vmem],
        out_specs=(hbm, hbm, hbm, vmem),
        scratch_shapes=[v((SHARE, FEAT), F32), v((HALF, WIDTH), F32), v((HALF, WIDTH), F32), dma((2, 6))],
    )(*made)
    return hidden[None], keys[None], values[None], rms


def solution(mesh):
    return jax.shard_map(
        per_device,
        mesh=mesh,
        in_specs=(
            P("vis", None, "row"),
            P("vis", "col", "row"),
            P(),
            P("vis", None),
            P("vis", None),
            P("row"),
            P("row", None, "col"),
            P("col", "row"),
            P("vis", None, "row", "col"),
            P("vis", None, "row", "col"),
        ),
        out_specs=(
            P("vis", "col", "row"),
            P("vis", "row", "col"),
            P("vis", "row", "col"),
            P("vis", None),
        ),
        check_vma=False,
    )
```

```python
import functools

import jax
import jax.numpy as jnp
from jax import lax
from jax.experimental import pallas as pl
from jax.experimental.pallas import tpu as pltpu
from jax.sharding import PartitionSpec as P

D = 5120
HD = 128
EPSILON = 1e-06
MASKED = -1e30
SCALE_LOG2E = HD ** (-0.5) * 1.4426950408889634

MESH = pl.DeviceIdType.MESH
F32 = jnp.float32
BF16 = jnp.bfloat16

COLS = 4
ZS = 8
YS = 4
TOK = 256
FEAT = 2560
QUART = 640
WIDTH = 1280
HEADS_HERE = 10
CACHE = 512
REQS = 4
HALF = 128
SHARE = 64
LOW = SHARE // 2
TILE = 1280
TILES = FEAT // TILE
Z_ORDER = (0, 1, 7, 2, 6, 3, 5, 4)


def nt_dot(left, right):
    return lax.dot_general(left, right, (((1,), (1,)), ((), ())), preferred_element_type=F32)


def nn_dot(left, right):
    return jnp.dot(left, right, preferred_element_type=F32)


def kernel(
    text_hbm, image_hbm, slots_ref, seg_ref, lens_ref, gain_ref, w_hbm, ow_hbm, ck_hbm, cv_hbm,
    hid_ref, nk_ref, nv_ref, rms_ref,
    w, ow, ck, cv, fill, gath, zsend, compact, scaled, gain, acc,
    sq_own, sq_peer, inv, kv_send, kv_recv, q_send, q_recv, q_bf, kv_bf,
    ext, onehot_t, bias_t, onehot, bias, scores, weights, o_own, o_peer, st_own, st_peer, att,
    to_across, to_right, to_left, from_across, from_left, from_right,
    w_sem, in_sem, xy_send, xy_recv, z_send, z_recv, x_send, x_recv,
    pr_send, pr_recv, o_send, o_recv, r_send, r_recv,
):
    row = lax.axis_index("row")
    col = lax.axis_index("col")
    vis = lax.axis_index("vis")
    z = lax.div(vis, YS)
    y = lax.rem(vis, YS)
    other = 1 - row
    right = lax.rem(col + 1, COLS)
    left = lax.rem(col + COLS - 1, COLS)
    across = lax.rem(col + 2, COLS)

    def at(r, c, v):
        return (r, c, v)

    block = y * COLS + col
    barrier = pltpu.get_barrier_semaphore()
    for step in (4, 3, 5, 2, 6, 1, 7):
        pl.semaphore_signal(
            barrier, inc=1, device_id=at(row, col, lax.rem(z + step, ZS) * YS + y), device_id_type=MESH)
    for step in range(1, 16):
        to = lax.rem(block + step, 16)
        pl.semaphore_signal(
            barrier, inc=1, device_id=at(row, lax.rem(to, COLS), z * YS + lax.div(to, COLS)), device_id_type=MESH)
    pl.semaphore_signal(barrier, inc=1, device_id=at(other, col, vis), device_id_type=MESH)
    loads_w = []
    for j in (1, 2, 0):
        for part in range(4):
            rows = pl.ds(part * QUART, QUART)
            cp = pltpu.make_async_copy(w_hbm.at[j, rows], w.at[j, rows], w_sem.at[j * 4 + part])
            loads_w.append((j, cp))
    load_text = pltpu.make_async_copy(text_hbm, fill, in_sem.at[0])
    load_k = [pltpu.make_async_copy(ck_hbm.at[s], ck.at[s], in_sem.at[1 + s]) for s in range(REQS)]
    load_v = [pltpu.make_async_copy(cv_hbm.at[s], cv.at[s], in_sem.at[5 + s]) for s in range(REQS)]
    load_ow = [
        pltpu.make_async_copy(ow_hbm.at[pl.ds(p * 320, 320)], ow.at[pl.ds(p * 320, 320)], in_sem.at[9 + p])
        for p in range(4)
    ]
    own_rows = pl.ds(pl.multiple_of(block * 16, 16), 16)
    own_cols = pl.ds(pl.multiple_of(col * QUART, 128), QUART)
    load_own = pltpu.make_async_copy(image_hbm.at[:, own_cols], gath.at[own_rows], in_sem.at[13])
    load_own.start()
    load_text.start()

    pl.semaphore_wait(barrier, 23)
    for step in range(1, 16):
        to = lax.rem(block + step, 16)
        to_col = lax.rem(to, COLS)
        pltpu.make_async_remote_copy(
            src_ref=image_hbm.at[:, pl.ds(pl.multiple_of(to_col * QUART, 128), QUART)],
            dst_ref=gath.at[own_rows],
            send_sem=xy_send.at[step], recv_sem=xy_recv.at[step],
            device_id=at(row, to_col, z * YS + lax.div(to, COLS)), device_id_type=MESH).start()
    for _, cp in loads_w:
        cp.start()

    load_text.wait()
    for k in range(FEAT // HD):
        gain[:, k * HD:(k + 1) * HD] = jnp.broadcast_to(gain_ref[pl.ds(k * HD, HD)].reshape(1, HD), (8, HD))

    lane256 = lax.broadcasted_iota(jnp.int32, (128, TOK), 1)
    sub128 = lax.broadcasted_iota(jnp.int32, (128, TOK), 0)
    before = jnp.where(
        lax.broadcasted_iota(jnp.int32, (TOK, TOK), 0) < lax.broadcasted_iota(jnp.int32, (TOK, TOK), 1), 1.0, 0.0
    ).astype(BF16)
    to_rows = jnp.concatenate(
        [jnp.broadcast_to(slots_ref[pl.ds(zz * YS + y, 1), :], (16, TOK)) for zz in range(ZS)], axis=0)
    rank_of = sub128 & 3
    match = (to_rows >> 6) == (z * YS + ((sub128 & 15) >> 2))
    earlier = nn_dot(jnp.where(match, 1.0, 0.0).astype(BF16), before)
    chosen = match & (earlier.astype(jnp.int32) == rank_of)
    token_at = jnp.sum(
        jnp.where(chosen, (to_rows - z * TOK + 1).astype(F32), 0.0), axis=1, keepdims=True).astype(jnp.int32) - 1
    select = jnp.where(token_at == lane256, 1.0, 0.0).astype(BF16)

    here_rows = jnp.broadcast_to(slots_ref[pl.ds(vis, 1), :], (128, TOK))
    slab = sub128 >> 4
    offset = jnp.zeros_like(slab)
    for i, dz in enumerate(Z_ORDER):
        offset = jnp.where(slab == i, dz, offset)
    here = (here_rows >> 6) == (((z + offset) & (ZS - 1)) * YS + ((sub128 & 15) >> 2))
    here_before = nn_dot(jnp.where(here, 1.0, 0.0).astype(BF16), before)
    place_f = jnp.where(here & (here_before.astype(jnp.int32) == rank_of), 1.0, 0.0).T
    place = place_f.astype(BF16)
    has_image = jnp.sum(place_f, axis=1, keepdims=True)

    seg_rows = jnp.broadcast_to(seg_ref[...], (128, TOK))
    oh = jnp.where(seg_rows == sub128, 1.0, 0.0).T
    onehot_t[...] = oh.astype(BF16)
    lane128 = lax.broadcasted_iota(jnp.int32, (TOK, HALF), 1)
    tok128 = lax.broadcasted_iota(jnp.int32, (TOK, HALF), 0)
    seg_col = jnp.sum(oh * lane128.astype(F32), axis=1, keepdims=True).astype(jnp.int32)
    seg_mine = jnp.where(row == 0, seg_ref[:, :HALF], seg_ref[:, HALF:])
    bias_t[...] = jnp.where(
        (seg_col == seg_mine) & (lane128 + row * HALF <= tok128), 0.0, MASKED)
    spans = (
        (across * SHARE, SHARE), (right * SHARE, LOW), (left * SHARE, LOW),
        (right * SHARE + LOW, LOW), (left * SHARE + LOW, LOW), (col * SHARE, SHARE),
    )
    moves = []
    for start, count in spans:
        first = sum(m[2] for m in moves)
        moves.append((pl.ds(pl.multiple_of(start, LOW), count), slice(first, first + count), count))
    for src, dst, _ in moves:
        onehot[dst, :] = onehot_t[src, :]
        bias[dst, :] = bias_t[src, :]
    for s in range(REQS):
        lane_c = lax.broadcasted_iota(jnp.int32, (CACHE, HD), 1)
        pos = lax.broadcasted_iota(jnp.int32, (CACHE, HD), 0) + row * CACHE
        seen = (lane_c == s) & (pos < lens_ref[0, s])
        ext[s] = jnp.where(seen | (lane_c >= REQS), 0.0, MASKED).astype(BF16)

    load_own.wait()
    for step in range(1, 16):
        frm = lax.rem(block + 16 - step, 16)
        rows = pl.ds(pl.multiple_of(frm * 16, 16), 16)
        pltpu.make_async_remote_copy(
            src_ref=gath.at[rows], dst_ref=gath.at[rows],
            send_sem=xy_send.at[step], recv_sem=xy_recv.at[step],
            device_id=at(row, col, vis), device_id_type=MESH).wait_recv()

    def block_at(dz):
        return compact.at[pl.ds(Z_ORDER.index(dz) * 16, 16), own_cols]

    picked_rows = nn_dot(select, gath[...]).astype(BF16)
    zsend[...] = picked_rows
    for dz in Z_ORDER[1:]:
        zz = lax.rem(z + dz, ZS)
        pltpu.make_async_remote_copy(
            src_ref=zsend.at[pl.ds(pl.multiple_of(zz * 16, 16), 16)],
            dst_ref=block_at(ZS - dz),
            send_sem=z_send.at[dz], recv_sem=z_recv.at[ZS - dz],
            device_id=at(row, col, zz * YS + y), device_id_type=MESH).start()
    block_own = pltpu.make_async_copy(
        zsend.at[pl.ds(pl.multiple_of(z * 16, 16), 16)], block_at(0), in_sem.at[14])
    block_own.start()
    for group in (load_k, load_v, load_ow):
        for cp in group:
            cp.start()

    def quarter(c_src):
        return pl.ds(pl.multiple_of(c_src * QUART, 128), QUART)

    def x_copy(c_src, to_col, lane):
        rows = pl.ds(0, 128) if lane == 4 else pl.ds(lane % 2 * 64, 64)
        part = compact.at[rows, quarter(c_src)]
        return pltpu.make_async_remote_copy(
            src_ref=part, dst_ref=part, send_sem=x_send.at[lane], recv_sem=x_recv.at[lane],
            device_id=at(row, to_col, vis), device_id_type=MESH)

    x_sends = [x_copy(col, right if lane < 2 else left, lane) for lane in range(4)] + [x_copy(col, across, 4)]
    block_own.wait()
    for i, dz in enumerate(Z_ORDER):
        if i > 0:
            pltpu.make_async_remote_copy(
                src_ref=block_at(dz), dst_ref=block_at(dz),
                send_sem=z_send.at[dz], recv_sem=z_recv.at[dz],
                device_id=at(row, col, vis), device_id_type=MESH).wait_recv()
        if i == 3:
            x_sends[0].start()
            x_sends[2].start()
    x_sends[1].start()
    x_sends[3].start()

    def to_peer(src, dst, k):
        return pltpu.make_async_remote_copy(
            src_ref=src, dst_ref=dst, send_sem=pr_send.at[k], recv_sem=pr_recv.at[k],
            device_id=at(other, col, vis), device_id_type=MESH)

    def fill_quarter(c_src, squares):
        cols = quarter(c_src)
        rows_f = jnp.where(has_image > 0.0, nn_dot(place, compact[:, cols]), fill[:, cols].astype(F32))
        fill[:, cols] = rows_f.astype(BF16)
        scaled[:, cols] = (rows_f * gain[0:1, cols]).astype(BF16)
        for k in range(QUART // HD):
            piece = rows_f[:, k * HD:(k + 1) * HD]
            squares = squares + piece * piece
        return squares

    def product(c_src, j):
        return nn_dot(scaled[:, quarter(c_src)], w[j, quarter(c_src), :])

    def out_cols(j):
        return slice(j * WIDTH, (j + 1) * WIDTH)

    squares = fill_quarter(col, jnp.zeros((TOK, HD), F32))
    for jj, cp in loads_w:
        cp.wait()
    for j in range(3):
        acc[:, out_cols(j)] = product(col, j)
    for cp in x_sends[:4]:
        cp.wait_send()
    x_sends[4].start()
    for c_src, lane in ((left, 0), (right, 2)):
        x_copy(c_src, across, lane).wait_recv()
        x_copy(c_src, across, lane + 1).wait_recv()
        squares = fill_quarter(c_src, squares)
    for j in range(3):
        acc[:, out_cols(j)] += product(left, j)
        acc[:, out_cols(j)] += product(right, j)
    x_copy(across, right, 4).wait_recv()
    squares = fill_quarter(across, squares)
    sq_own[...] = jnp.broadcast_to(jnp.sum(squares, axis=1, keepdims=True), (TOK, HD))
    sq_copy = to_peer(sq_own, sq_peer, 0)
    sq_copy.start()
    peer_copies = {0: to_peer(q_send, q_recv, 3)}
    acc[:, out_cols(0)] += product(across, 0)
    q_send[...] = acc[:, out_cols(0)].astype(BF16)
    peer_copies[0].start()
    my_rows = pl.ds(pl.multiple_of(row * HALF, HALF), HALF)
    its_rows = pl.ds(pl.multiple_of(other * HALF, HALF), HALF)
    for j in (1, 2):
        acc[:, out_cols(j)] += product(across, j)
        kv_send[j - 1] = acc[its_rows, out_cols(j)].astype(BF16)
        peer_copies[j] = to_peer(kv_send.at[j - 1], kv_recv.at[j - 1], j)
        peer_copies[j].start()

    sq_copy.wait()
    total_sq = sq_own[...] + sq_peer[...]
    inv[...] = lax.rsqrt(total_sq / D + EPSILON)
    per_request = jnp.sum(oh * total_sq, axis=0, keepdims=True)
    counts = jnp.sum(oh, axis=0, keepdims=True)
    rms_ref[...] = jnp.sqrt(per_request / (counts * D))[:, :REQS]
    inv_mine = inv[my_rows, :]
    peer_copies[0].wait()
    for src, dst, _ in moves:
        inv_rows = inv[src, :]
        for h in range(HEADS_HERE):
            lanes = slice(h * HD, (h + 1) * HD)
            q_bf[dst, lanes] = ((acc[src, lanes] + q_recv[src, lanes].astype(F32)) * inv_rows).astype(BF16)

    def finish_new(j, dst):
        peer_copies[j].wait()
        for h in range(HEADS_HERE):
            lanes = slice(h * HD, (h + 1) * HD)
            value = (acc[my_rows, j * WIDTH + h * HD:j * WIDTH + (h + 1) * HD] + kv_recv[j - 1, :, lanes].astype(F32)) * inv_mine
            dst[:, lanes] = value
            kv_bf[j - 1, :, lanes] = value.astype(BF16)

    finish_new(1, nk_ref)

    for group in (load_k, load_v):
        for cp in group:
            cp.wait()
    st_own[...] = jnp.zeros((TOK, HD), F32)

    def rows_of(part):
        return slice(part * HALF, (part + 1) * HALF)

    def o_copy(part, h):
        where = (pl.ds(part * HALF, HALF), pl.ds(pl.multiple_of(h * HD, HD), HD))
        return pltpu.make_async_remote_copy(
            src_ref=o_own.at[where], dst_ref=o_peer.at[where],
            send_sem=o_send.at[part, h], recv_sem=o_recv.at[part, h],
            device_id=at(other, col, vis), device_id_type=MESH)

    def st_copy(part):
        where = pl.ds(part * HALF, HALF)
        return to_peer(st_own.at[where], st_peer.at[where], 4 + part)

    def weigh(part, h):
        lanes = pl.ds(pl.multiple_of(h * HD, HD), HD)
        q = q_bf[rows_of(part), lanes]
        q_ext = jnp.concatenate([q, onehot[rows_of(part), :]], axis=1)
        peak = nt_dot(q, kv_bf[0, :, lanes]) + bias[rows_of(part), :]
        scores[:, REQS * CACHE:] = peak
        for s in range(REQS):
            piece = nt_dot(q_ext, jnp.concatenate([ck[s, :, lanes], ext[s]], axis=1))
            scores[:, s * CACHE:(s + 1) * CACHE] = piece
            for k in range(CACHE // HD):
                peak = jnp.maximum(peak, piece[:, k * HD:(k + 1) * HD])
        top = jnp.max(peak, axis=1, keepdims=True) * SCALE_LOG2E
        weights[...] = jnp.exp2(scores[...] * SCALE_LOG2E - top).astype(BF16)
        return top

    lane_h = lax.broadcasted_iota(jnp.int32, (HALF, HD), 1)

    def gather_values(part, h, top):
        lanes = pl.ds(pl.multiple_of(h * HD, HD), HD)
        ones = jnp.ones((CACHE, HD), BF16)
        total_acc = nn_dot(
            weights[:, REQS * CACHE:], jnp.concatenate([kv_bf[1, :, lanes], ones[:HALF]], axis=1))
        for s in range(REQS):
            total_acc = total_acc + nn_dot(
                weights[:, s * CACHE:(s + 1) * CACHE], jnp.concatenate([cv[s, :, lanes], ones], axis=1))
        total = total_acc[:, HD:]
        o_own[rows_of(part), lanes] = (total_acc[:, :HD] / total).astype(BF16)
        st_own[rows_of(part), :] = jnp.where(lane_h == h, top + jnp.log2(total), st_own[rows_of(part), :])

    def all_heads(part, top):
        def head(h, top):
            gather_values(part, h, top)
            top = weigh(part, h + 1)
            o_copy(part, h).start()
            return top

        top = lax.fori_loop(0, HEADS_HERE - 1, head, top)
        gather_values(part, HEADS_HERE - 1, top)
        o_copy(part, HEADS_HERE - 1).start()
        st_copy(part).start()

    def join(part):
        st_copy(part).wait()
        lead = st_own[rows_of(part), :] - st_peer[rows_of(part), :]
        mine = 1.0 / (1.0 + jnp.exp2(-lead))
        theirs = 1.0 / (1.0 + jnp.exp2(lead))
        for h in range(HEADS_HERE):
            lanes = slice(h * HD, (h + 1) * HD)
            o_copy(part, h).wait()
            att[:, lanes] = (
                o_own[rows_of(part), lanes].astype(F32) * mine[:, h:h + 1]
                + o_peer[rows_of(part), lanes].astype(F32) * theirs[:, h:h + 1]
            ).astype(BF16)

    low, high = pl.ds(0, LOW), pl.ds(LOW, LOW)

    def ring(n, lane):
        src, dst, to_col = (
            (to_across.at[n], from_across.at[n], across),
            (to_right.at[n, low], from_left.at[n, low], right),
            (to_left.at[n, low], from_right.at[n, low], left),
            (to_right.at[n, high], from_left.at[n, high], right),
            (to_left.at[n, high], from_right.at[n, high], left),
        )[lane]
        return pltpu.make_async_remote_copy(
            src_ref=src, dst_ref=dst, send_sem=r_send.at[n, lane], recv_sem=r_recv.at[n, lane],
            device_id=at(row, to_col, vis), device_id_type=MESH)

    top = weigh(0, 0)
    finish_new(2, nv_ref)
    all_heads(0, top)
    top = weigh(1, 0)
    join(0)
    for cp in load_ow:
        cp.wait()
    for n in range(TILES):
        piece = nn_dot(att[...], ow[:, n * TILE:(n + 1) * TILE])
        to_across[n] = piece[:SHARE].astype(BF16)
        ring(n, 0).start()
        to_right[n, :LOW] = piece[SHARE:SHARE + LOW].astype(BF16)
        to_left[n, :LOW] = piece[SHARE + LOW:].astype(BF16)
        ring(n, 1).start()
        ring(n, 2).start()
    all_heads(1, top)
    join(1)
    for n in range(TILES):
        piece = nn_dot(att[...], ow[:, n * TILE:(n + 1) * TILE])
        to_right[n, LOW:] = piece[:LOW].astype(BF16)
        to_left[n, LOW:] = piece[LOW:SHARE].astype(BF16)
        ring(n, 3).start()
        ring(n, 4).start()
        acc[:SHARE, n * TILE:(n + 1) * TILE] = piece[SHARE:]
    own_share = pl.ds(pl.multiple_of(col * SHARE, SHARE), SHARE)
    for n in range(TILES):
        cols = slice(n * TILE, (n + 1) * TILE)
        for lane in range(5):
            ring(n, lane).wait_recv()
        hid_ref[:, cols] = (
            fill[own_share, cols].astype(F32) + acc[:SHARE, cols] + from_across[n].astype(F32)
            + (from_left[n].astype(F32) + from_right[n].astype(F32)))

    for step in range(1, 16):
        pltpu.make_async_remote_copy(
            src_ref=image_hbm.at[:, own_cols], dst_ref=gath.at[own_rows],
            send_sem=xy_send.at[step], recv_sem=xy_recv.at[step],
            device_id=at(other, col, vis), device_id_type=MESH).wait_send()
    for dz in Z_ORDER[1:]:
        pltpu.make_async_remote_copy(
            src_ref=zsend.at[pl.ds(0, 16)], dst_ref=block_at(0),
            send_sem=z_send.at[dz], recv_sem=z_recv.at[dz],
            device_id=at(other, col, vis), device_id_type=MESH).wait_send()
    x_sends[4].wait_send()
    for n in range(TILES):
        for lane in range(5):
            ring(n, lane).wait_send()


def per_device(
    text_embed, image_embed, slot_source, segment_ids, prefix_lengths,
    attn_gain, qkv_weight, out_weight, cache_keys, cache_values,
):
    hbm = pl.BlockSpec(memory_space=pl.ANY)
    vmem = pl.BlockSpec(memory_space=pltpu.VMEM)
    smem = pl.BlockSpec(memory_space=pltpu.SMEM)

    def v(shape, dtype):
        return pltpu.VMEM(shape, dtype)

    dma = pltpu.SemaphoreType.DMA
    results = (
        jax.ShapeDtypeStruct((SHARE, FEAT), F32),
        jax.ShapeDtypeStruct((HALF, WIDTH), F32),
        jax.ShapeDtypeStruct((HALF, WIDTH), F32),
        jax.ShapeDtypeStruct((1, REQS), F32),
    )
    made = pl.pallas_call(
        kernel,
        out_shape=tuple(v(r.shape, r.dtype) for r in results),
        in_specs=[hbm, hbm, vmem, vmem, smem, vmem, hbm, hbm, hbm, hbm],
        out_specs=(vmem, vmem, vmem, vmem),
        scratch_shapes=[
            v((3, FEAT, WIDTH), BF16), v((WIDTH, FEAT), BF16),
            v((REQS, CACHE, WIDTH), BF16), v((REQS, CACHE, WIDTH), BF16),
            v((TOK, FEAT), BF16), v((TOK, QUART), BF16), v((HALF, QUART), BF16), v((HALF, FEAT), BF16),
            v((TOK, FEAT), BF16), v((8, FEAT), F32), v((TOK, 3 * WIDTH), F32),
            v((TOK, HD), F32), v((TOK, HD), F32), v((TOK, HD), F32),
            v((2, HALF, WIDTH), BF16), v((2, HALF, WIDTH), BF16),
            v((TOK, WIDTH), BF16), v((TOK, WIDTH), BF16), v((TOK, WIDTH), BF16),
            v((2, HALF, WIDTH), BF16),
            v((REQS, CACHE, HD), BF16), v((TOK, HD), BF16), v((TOK, HALF), F32),
            v((TOK, HD), BF16), v((TOK, HALF), F32),
            v((HALF, REQS * CACHE + HALF), F32), v((HALF, REQS * CACHE + HALF), BF16),
            v((TOK, WIDTH), BF16), v((TOK, WIDTH), BF16), v((TOK, HD), F32), v((TOK, HD), F32),
            v((HALF, WIDTH), BF16),
            v((TILES, SHARE, TILE), BF16), v((TILES, SHARE, TILE), BF16), v((TILES, SHARE, TILE), BF16),
            v((TILES, SHARE, TILE), BF16), v((TILES, SHARE, TILE), BF16), v((TILES, SHARE, TILE), BF16),
            dma((12,)), dma((15,)), dma((16,)), dma((16,)), dma((8,)), dma((8,)),
            dma((5,)), dma((5,)), dma((6,)), dma((6,)), dma((2, HEADS_HERE)), dma((2, HEADS_HERE)),
            dma((TILES, 5)), dma((TILES, 5)),
        ],
        compiler_params=pltpu.CompilerParams(
            collective_id=0, has_side_effects=True, vmem_limit_bytes=60 * 1024 * 1024),
    )(
        text_embed[0], image_embed[0], slot_source, segment_ids, prefix_lengths,
        attn_gain, qkv_weight.transpose(1, 0, 2), out_weight, cache_keys[0], cache_values[0],
    )
    hidden, keys, values, rms = made
    return hidden[None], keys[None], values[None], rms


def solution(mesh):
    return jax.shard_map(
        per_device,
        mesh=mesh,
        in_specs=(
            P("vis", None, "row"),
            P("vis", "col", "row"),
            P(),
            P("vis", None),
            P("vis", None),
            P("row"),
            P("row", None, "col"),
            P("col", "row"),
            P("vis", None, "row", "col"),
            P("vis", None, "row", "col"),
        ),
        out_specs=(
            P("vis", "col", "row"),
            P("vis", "row", "col"),
            P("vis", "row", "col"),
            P("vis", None),
        ),
        check_vma=False,
    )
```

```python
import functools

import jax
import jax.numpy as jnp
from jax import lax
from jax.experimental import pallas as pl
from jax.experimental.pallas import tpu as pltpu
from jax.sharding import PartitionSpec as P

D = 5120
HD = 128
EPSILON = 1e-06
MASKED = -1e30
SCALE_LOG2E = HD ** (-0.5) * 1.4426950408889634

MESH = pl.DeviceIdType.MESH
F32 = jnp.float32
BF16 = jnp.bfloat16

COLS = 4
ZS = 8
YS = 4
TOK = 256
FEAT = 2560
QUART = 640
WIDTH = 1280
HEADS_HERE = 10
CACHE = 512
REQS = 4
HALF = 128
SHARE = 64
LOW = SHARE // 2
TILE = 1280
TILES = FEAT // TILE
Z_ORDER = (0, 1, 7, 2, 6, 3, 5, 4)


def nt_dot(left, right):
    return lax.dot_general(left, right, (((1,), (1,)), ((), ())), preferred_element_type=F32)


def nn_dot(left, right):
    return jnp.dot(left, right, preferred_element_type=F32)


def kernel(
    text_hbm, image_hbm, slots_ref, seg_ref, lens_ref, gain_ref, w_hbm, ow_hbm, ck_hbm, cv_hbm,
    hid_ref, nk_ref, nv_ref, rms_ref,
    w, ow, ck, cv, fill, gath, zsend, compact, scaled, gain, acc,
    sq_own, sq_peer, inv, kv_send, kv_recv, q_send, q_recv, q_bf, kv_bf,
    ext, onehot_t, bias_t, onehot, bias, scores, weights, o_own, o_peer, st_own, st_peer, att,
    to_across, to_right, to_left, from_across, from_left, from_right,
    w_sem, in_sem, xy_send, xy_recv, z_send, z_recv, x_send, x_recv,
    pr_send, pr_recv, o_send, o_recv, r_send, r_recv,
):
    row = lax.axis_index("row")
    col = lax.axis_index("col")
    vis = lax.axis_index("vis")
    z = lax.div(vis, YS)
    y = lax.rem(vis, YS)
    other = 1 - row
    right = lax.rem(col + 1, COLS)
    left = lax.rem(col + COLS - 1, COLS)
    across = lax.rem(col + 2, COLS)

    def at(r, c, v):
        return (r, c, v)

    block = y * COLS + col
    barrier = pltpu.get_barrier_semaphore()
    for step in (4, 3, 5, 2, 6, 1, 7):
        pl.semaphore_signal(
            barrier, inc=1, device_id=at(row, col, lax.rem(z + step, ZS) * YS + y), device_id_type=MESH)
    for step in range(1, 16):
        to = lax.rem(block + step, 16)
        pl.semaphore_signal(
            barrier, inc=1, device_id=at(row, lax.rem(to, COLS), z * YS + lax.div(to, COLS)), device_id_type=MESH)
    pl.semaphore_signal(barrier, inc=1, device_id=at(other, col, vis), device_id_type=MESH)
    loads_w = []
    for j in (1, 2, 0):
        for part in range(4):
            rows = pl.ds(part * QUART, QUART)
            cp = pltpu.make_async_copy(w_hbm.at[j, rows], w.at[j, rows], w_sem.at[j * 4 + part])
            loads_w.append((j, cp))
    load_text = pltpu.make_async_copy(text_hbm, fill, in_sem.at[0])
    load_k = [pltpu.make_async_copy(ck_hbm.at[s], ck.at[s], in_sem.at[1 + s]) for s in range(REQS)]
    load_v = [pltpu.make_async_copy(cv_hbm.at[s], cv.at[s], in_sem.at[5 + s]) for s in range(REQS)]
    load_ow = [
        pltpu.make_async_copy(ow_hbm.at[pl.ds(p * 320, 320)], ow.at[pl.ds(p * 320, 320)], in_sem.at[9 + p])
        for p in range(4)
    ]
    own_rows = pl.ds(pl.multiple_of(block * 16, 16), 16)
    own_cols = pl.ds(pl.multiple_of(col * QUART, 128), QUART)
    load_own = pltpu.make_async_copy(image_hbm.at[:, own_cols], gath.at[own_rows], in_sem.at[13])
    load_own.start()
    load_text.start()

    pl.semaphore_wait(barrier, 23)
    for step in range(1, 16):
        to = lax.rem(block + step, 16)
        to_col = lax.rem(to, COLS)
        pltpu.make_async_remote_copy(
            src_ref=image_hbm.at[:, pl.ds(pl.multiple_of(to_col * QUART, 128), QUART)],
            dst_ref=gath.at[own_rows],
            send_sem=xy_send.at[step], recv_sem=xy_recv.at[step],
            device_id=at(row, to_col, z * YS + lax.div(to, COLS)), device_id_type=MESH).start()
    for _, cp in loads_w:
        cp.start()

    load_text.wait()
    for k in range(FEAT // HD):
        gain[:, k * HD:(k + 1) * HD] = jnp.broadcast_to(gain_ref[pl.ds(k * HD, HD)].reshape(1, HD), (8, HD))

    lane256 = lax.broadcasted_iota(jnp.int32, (128, TOK), 1)
    sub128 = lax.broadcasted_iota(jnp.int32, (128, TOK), 0)
    before = jnp.where(
        lax.broadcasted_iota(jnp.int32, (TOK, TOK), 0) < lax.broadcasted_iota(jnp.int32, (TOK, TOK), 1), 1.0, 0.0
    ).astype(BF16)
    to_rows = jnp.concatenate(
        [jnp.broadcast_to(slots_ref[pl.ds(zz * YS + y, 1), :], (16, TOK)) for zz in range(ZS)], axis=0)
    rank_of = sub128 & 3
    match = (to_rows >> 6) == (z * YS + ((sub128 & 15) >> 2))
    earlier = nn_dot(jnp.where(match, 1.0, 0.0).astype(BF16), before)
    chosen = match & (earlier.astype(jnp.int32) == rank_of)
    token_at = jnp.sum(
        jnp.where(chosen, (to_rows - z * TOK + 1).astype(F32), 0.0), axis=1, keepdims=True).astype(jnp.int32) - 1
    select = jnp.where(token_at == lane256, 1.0, 0.0).astype(BF16)

    here_rows = jnp.broadcast_to(slots_ref[pl.ds(vis, 1), :], (128, TOK))
    slab = sub128 >> 4
    offset = jnp.zeros_like(slab)
    for i, dz in enumerate(Z_ORDER):
        offset = jnp.where(slab == i, dz, offset)
    here = (here_rows >> 6) == (((z + offset) & (ZS - 1)) * YS + ((sub128 & 15) >> 2))
    here_before = nn_dot(jnp.where(here, 1.0, 0.0).astype(BF16), before)
    place_f = jnp.where(here & (here_before.astype(jnp.int32) == rank_of), 1.0, 0.0).T
    place = place_f.astype(BF16)
    has_image = jnp.sum(place_f, axis=1, keepdims=True)

    seg_rows = jnp.broadcast_to(seg_ref[...], (128, TOK))
    oh = jnp.where(seg_rows == sub128, 1.0, 0.0).T
    onehot_t[...] = oh.astype(BF16)
    lane128 = lax.broadcasted_iota(jnp.int32, (TOK, HALF), 1)
    tok128 = lax.broadcasted_iota(jnp.int32, (TOK, HALF), 0)
    seg_col = jnp.sum(oh * lane128.astype(F32), axis=1, keepdims=True).astype(jnp.int32)
    seg_mine = jnp.where(row == 0, seg_ref[:, :HALF], seg_ref[:, HALF:])
    bias_t[...] = jnp.where(
        (seg_col == seg_mine) & (lane128 + row * HALF <= tok128), 0.0, MASKED)
    spans = (
        (across * SHARE, SHARE), (right * SHARE, LOW), (left * SHARE, LOW),
        (right * SHARE + LOW, LOW), (left * SHARE + LOW, LOW), (col * SHARE, SHARE),
    )
    moves = []
    for start, count in spans:
        first = sum(m[2] for m in moves)
        moves.append((pl.ds(pl.multiple_of(start, LOW), count), slice(first, first + count), count))
    for src, dst, _ in moves:
        onehot[dst, :] = onehot_t[src, :]
        bias[dst, :] = bias_t[src, :]
    for s in range(REQS):
        lane_c = lax.broadcasted_iota(jnp.int32, (CACHE, HD), 1)
        pos = lax.broadcasted_iota(jnp.int32, (CACHE, HD), 0) + row * CACHE
        seen = (lane_c == s) & (pos < lens_ref[0, s])
        ext[s] = jnp.where(seen | (lane_c >= REQS), 0.0, MASKED).astype(BF16)

    load_own.wait()
    for step in range(1, 16):
        frm = lax.rem(block + 16 - step, 16)
        rows = pl.ds(pl.multiple_of(frm * 16, 16), 16)
        pltpu.make_async_remote_copy(
            src_ref=gath.at[rows], dst_ref=gath.at[rows],
            send_sem=xy_send.at[step], recv_sem=xy_recv.at[step],
            device_id=at(row, col, vis), device_id_type=MESH).wait_recv()

    def block_at(dz):
        return compact.at[pl.ds(Z_ORDER.index(dz) * 16, 16), own_cols]

    picked_rows = nn_dot(select, gath[...]).astype(BF16)
    zsend[...] = picked_rows
    for dz in Z_ORDER[1:]:
        zz = lax.rem(z + dz, ZS)
        pltpu.make_async_remote_copy(
            src_ref=zsend.at[pl.ds(pl.multiple_of(zz * 16, 16), 16)],
            dst_ref=block_at(ZS - dz),
            send_sem=z_send.at[dz], recv_sem=z_recv.at[ZS - dz],
            device_id=at(row, col, zz * YS + y), device_id_type=MESH).start()
    block_own = pltpu.make_async_copy(
        zsend.at[pl.ds(pl.multiple_of(z * 16, 16), 16)], block_at(0), in_sem.at[14])
    block_own.start()
    for group in (load_k, load_v, load_ow):
        for cp in group:
            cp.start()

    def quarter(c_src):
        return pl.ds(pl.multiple_of(c_src * QUART, 128), QUART)

    def x_copy(c_src, to_col, lane):
        rows = pl.ds(0, 128) if lane == 4 else pl.ds(lane % 2 * 64, 64)
        part = compact.at[rows, quarter(c_src)]
        return pltpu.make_async_remote_copy(
            src_ref=part, dst_ref=part, send_sem=x_send.at[lane], recv_sem=x_recv.at[lane],
            device_id=at(row, to_col, vis), device_id_type=MESH)

    x_sends = [x_copy(col, right if lane < 2 else left, lane) for lane in range(4)] + [x_copy(col, across, 4)]
    block_own.wait()
    for i, dz in enumerate(Z_ORDER):
        if i > 0:
            pltpu.make_async_remote_copy(
                src_ref=block_at(dz), dst_ref=block_at(dz),
                send_sem=z_send.at[dz], recv_sem=z_recv.at[dz],
                device_id=at(row, col, vis), device_id_type=MESH).wait_recv()
        if i == 3:
            x_sends[0].start()
            x_sends[2].start()
    x_sends[1].start()
    x_sends[3].start()

    def to_peer(src, dst, k):
        return pltpu.make_async_remote_copy(
            src_ref=src, dst_ref=dst, send_sem=pr_send.at[k], recv_sem=pr_recv.at[k],
            device_id=at(other, col, vis), device_id_type=MESH)

    def fill_quarter(c_src, squares):
        cols = quarter(c_src)
        rows_f = jnp.where(has_image > 0.0, nn_dot(place, compact[:, cols]), fill[:, cols].astype(F32))
        fill[:, cols] = rows_f.astype(BF16)
        scaled[:, cols] = (rows_f * gain[0:1, cols]).astype(BF16)
        for k in range(QUART // HD):
            piece = rows_f[:, k * HD:(k + 1) * HD]
            squares = squares + piece * piece
        return squares

    def product(c_src, j):
        return nn_dot(scaled[:, quarter(c_src)], w[j, quarter(c_src), :])

    def out_cols(j):
        return slice(j * WIDTH, (j + 1) * WIDTH)

    squares = fill_quarter(col, jnp.zeros((TOK, HD), F32))
    for jj, cp in loads_w:
        cp.wait()
    for j in range(3):
        acc[:, out_cols(j)] = product(col, j)
    for cp in x_sends[:4]:
        cp.wait_send()
    x_sends[4].start()
    for c_src, lane in ((left, 0), (right, 2)):
        x_copy(c_src, across, lane).wait_recv()
        x_copy(c_src, across, lane + 1).wait_recv()
        squares = fill_quarter(c_src, squares)
    for j in range(3):
        acc[:, out_cols(j)] += product(left, j)
        acc[:, out_cols(j)] += product(right, j)
    x_copy(across, right, 4).wait_recv()
    squares = fill_quarter(across, squares)
    sq_own[...] = jnp.broadcast_to(jnp.sum(squares, axis=1, keepdims=True), (TOK, HD))
    sq_copy = to_peer(sq_own, sq_peer, 0)
    sq_copy.start()
    peer_copies = {0: to_peer(q_send, q_recv, 3)}
    acc[:, out_cols(0)] += product(across, 0)
    q_send[...] = acc[:, out_cols(0)].astype(BF16)
    peer_copies[0].start()
    my_rows = pl.ds(pl.multiple_of(row * HALF, HALF), HALF)
    its_rows = pl.ds(pl.multiple_of(other * HALF, HALF), HALF)
    for j in (1, 2):
        acc[:, out_cols(j)] += product(across, j)
        kv_send[j - 1] = acc[its_rows, out_cols(j)].astype(BF16)
        peer_copies[j] = to_peer(kv_send.at[j - 1], kv_recv.at[j - 1], j)
        peer_copies[j].start()

    sq_copy.wait()
    total_sq = sq_own[...] + sq_peer[...]
    inv[...] = lax.rsqrt(total_sq / D + EPSILON)
    per_request = jnp.sum(oh * total_sq, axis=0, keepdims=True)
    counts = jnp.sum(oh, axis=0, keepdims=True)
    rms_ref[...] = jnp.sqrt(per_request / (counts * D))[:, :REQS]
    inv_mine = inv[my_rows, :]
    peer_copies[0].wait()
    for src, dst, _ in moves:
        inv_rows = inv[src, :]
        for h in range(HEADS_HERE):
            lanes = slice(h * HD, (h + 1) * HD)
            q_bf[dst, lanes] = ((acc[src, lanes] + q_recv[src, lanes].astype(F32)) * inv_rows).astype(BF16)

    def finish_new(j, dst):
        peer_copies[j].wait()
        for h in range(HEADS_HERE):
            lanes = slice(h * HD, (h + 1) * HD)
            value = (acc[my_rows, j * WIDTH + h * HD:j * WIDTH + (h + 1) * HD] + kv_recv[j - 1, :, lanes].astype(F32)) * inv_mine
            dst[:, lanes] = value
            kv_bf[j - 1, :, lanes] = value.astype(BF16)

    finish_new(1, nk_ref)

    for group in (load_k, load_v):
        for cp in group:
            cp.wait()
    st_own[...] = jnp.zeros((TOK, HD), F32)

    def rows_of(part):
        return slice(part * HALF, (part + 1) * HALF)

    def o_copy(part, h):
        where = (pl.ds(part * HALF, HALF), pl.ds(pl.multiple_of(h * HD, HD), HD))
        return pltpu.make_async_remote_copy(
            src_ref=o_own.at[where], dst_ref=o_peer.at[where],
            send_sem=o_send.at[part, h], recv_sem=o_recv.at[part, h],
            device_id=at(other, col, vis), device_id_type=MESH)

    def st_copy(part):
        where = pl.ds(part * HALF, HALF)
        return to_peer(st_own.at[where], st_peer.at[where], 4 + part)

    def weigh(part, h):
        lanes = pl.ds(pl.multiple_of(h * HD, HD), HD)
        q = q_bf[rows_of(part), lanes]
        q_ext = jnp.concatenate([q, onehot[rows_of(part), :]], axis=1)
        peak = nt_dot(q, kv_bf[0, :, lanes]) + bias[rows_of(part), :]
        scores[:, REQS * CACHE:] = peak
        for s in range(REQS):
            piece = nt_dot(q_ext, jnp.concatenate([ck[s, :, lanes], ext[s]], axis=1))
            scores[:, s * CACHE:(s + 1) * CACHE] = piece
            for k in range(CACHE // HD):
                peak = jnp.maximum(peak, piece[:, k * HD:(k + 1) * HD])
        top = jnp.max(peak, axis=1, keepdims=True) * SCALE_LOG2E
        weights[...] = jnp.exp2(scores[...] * SCALE_LOG2E - top).astype(BF16)
        return top

    lane_h = lax.broadcasted_iota(jnp.int32, (HALF, HD), 1)

    def gather_values(part, h, top):
        lanes = pl.ds(pl.multiple_of(h * HD, HD), HD)
        ones = jnp.ones((CACHE, HD), BF16)
        total_acc = nn_dot(
            weights[:, REQS * CACHE:], jnp.concatenate([kv_bf[1, :, lanes], ones[:HALF]], axis=1))
        for s in range(REQS):
            total_acc = total_acc + nn_dot(
                weights[:, s * CACHE:(s + 1) * CACHE], jnp.concatenate([cv[s, :, lanes], ones], axis=1))
        total = total_acc[:, HD:]
        o_own[rows_of(part), lanes] = (total_acc[:, :HD] / total).astype(BF16)
        st_own[rows_of(part), :] = jnp.where(lane_h == h, top + jnp.log2(total), st_own[rows_of(part), :])

    def all_heads(part, top):
        def head(h, top):
            gather_values(part, h, top)
            top = weigh(part, h + 1)
            o_copy(part, h).start()
            return top

        top = lax.fori_loop(0, HEADS_HERE - 1, head, top)
        gather_values(part, HEADS_HERE - 1, top)
        o_copy(part, HEADS_HERE - 1).start()
        st_copy(part).start()

    def join(part):
        st_copy(part).wait()
        lead = st_own[rows_of(part), :] - st_peer[rows_of(part), :]
        mine = 1.0 / (1.0 + jnp.exp2(-lead))
        theirs = 1.0 / (1.0 + jnp.exp2(lead))
        for h in range(HEADS_HERE):
            lanes = slice(h * HD, (h + 1) * HD)
            o_copy(part, h).wait()
            att[:, lanes] = (
                o_own[rows_of(part), lanes].astype(F32) * mine[:, h:h + 1]
                + o_peer[rows_of(part), lanes].astype(F32) * theirs[:, h:h + 1]
            ).astype(BF16)

    low, high = pl.ds(0, LOW), pl.ds(LOW, LOW)

    def ring(n, lane):
        src, dst, to_col = (
            (to_across.at[n], from_across.at[n], across),
            (to_right.at[n, low], from_left.at[n, low], right),
            (to_left.at[n, low], from_right.at[n, low], left),
            (to_right.at[n, high], from_left.at[n, high], right),
            (to_left.at[n, high], from_right.at[n, high], left),
        )[lane]
        return pltpu.make_async_remote_copy(
            src_ref=src, dst_ref=dst, send_sem=r_send.at[n, lane], recv_sem=r_recv.at[n, lane],
            device_id=at(row, to_col, vis), device_id_type=MESH)

    top = weigh(0, 0)
    finish_new(2, nv_ref)
    all_heads(0, top)
    top = weigh(1, 0)
    join(0)
    for cp in load_ow:
        cp.wait()
    for n in range(TILES):
        piece = nn_dot(att[...], ow[:, n * TILE:(n + 1) * TILE])
        to_across[n] = piece[:SHARE].astype(BF16)
        ring(n, 0).start()
        to_right[n, :LOW] = piece[SHARE:SHARE + LOW].astype(BF16)
        to_left[n, :LOW] = piece[SHARE + LOW:].astype(BF16)
        ring(n, 1).start()
        ring(n, 2).start()
    all_heads(1, top)
    join(1)
    for n in range(TILES):
        piece = nn_dot(att[...], ow[:, n * TILE:(n + 1) * TILE])
        to_right[n, LOW:] = piece[:LOW].astype(BF16)
        to_left[n, LOW:] = piece[LOW:SHARE].astype(BF16)
        ring(n, 3).start()
        ring(n, 4).start()
        acc[:SHARE, n * TILE:(n + 1) * TILE] = piece[SHARE:]
    own_share = pl.ds(pl.multiple_of(col * SHARE, SHARE), SHARE)
    for n in range(TILES):
        cols = slice(n * TILE, (n + 1) * TILE)
        for lane in range(5):
            ring(n, lane).wait_recv()
        hid_ref[:, cols] = (
            fill[own_share, cols].astype(F32) + acc[:SHARE, cols] + from_across[n].astype(F32)
            + (from_left[n].astype(F32) + from_right[n].astype(F32)))

    for step in range(1, 16):
        pltpu.make_async_remote_copy(
            src_ref=image_hbm.at[:, own_cols], dst_ref=gath.at[own_rows],
            send_sem=xy_send.at[step], recv_sem=xy_recv.at[step],
            device_id=at(other, col, vis), device_id_type=MESH).wait_send()
    for dz in Z_ORDER[1:]:
        pltpu.make_async_remote_copy(
            src_ref=zsend.at[pl.ds(0, 16)], dst_ref=block_at(0),
            send_sem=z_send.at[dz], recv_sem=z_recv.at[dz],
            device_id=at(other, col, vis), device_id_type=MESH).wait_send()
    x_sends[4].wait_send()
    for n in range(TILES):
        for lane in range(5):
            ring(n, lane).wait_send()


def hand_over(*refs):
    ins, outs, sems = refs[:4], refs[4:8], refs[8]
    copies = [pltpu.make_async_copy(ins[i], outs[i], sems.at[i]) for i in range(4)]
    for cp in copies:
        cp.start()
    for cp in copies:
        cp.wait()


def per_device(
    text_embed, image_embed, slot_source, segment_ids, prefix_lengths,
    attn_gain, qkv_weight, out_weight, cache_keys, cache_values,
):
    hbm = pl.BlockSpec(memory_space=pl.ANY)
    vmem = pl.BlockSpec(memory_space=pltpu.VMEM)
    smem = pl.BlockSpec(memory_space=pltpu.SMEM)

    def v(shape, dtype):
        return pltpu.VMEM(shape, dtype)

    dma = pltpu.SemaphoreType.DMA
    results = (
        jax.ShapeDtypeStruct((SHARE, FEAT), F32),
        jax.ShapeDtypeStruct((HALF, WIDTH), F32),
        jax.ShapeDtypeStruct((HALF, WIDTH), F32),
        jax.ShapeDtypeStruct((1, REQS), F32),
    )
    made = pl.pallas_call(
        kernel,
        out_shape=tuple(v(r.shape, r.dtype) for r in results),
        in_specs=[hbm, hbm, vmem, vmem, smem, vmem, hbm, hbm, hbm, hbm],
        out_specs=(vmem, vmem, vmem, vmem),
        scratch_shapes=[
            v((3, FEAT, WIDTH), BF16), v((WIDTH, FEAT), BF16),
            v((REQS, CACHE, WIDTH), BF16), v((REQS, CACHE, WIDTH), BF16),
            v((TOK, FEAT), BF16), v((TOK, QUART), BF16), v((HALF, QUART), BF16), v((HALF, FEAT), BF16),
            v((TOK, FEAT), BF16), v((8, FEAT), F32), v((TOK, 3 * WIDTH), F32),
            v((TOK, HD), F32), v((TOK, HD), F32), v((TOK, HD), F32),
            v((2, HALF, WIDTH), BF16), v((2, HALF, WIDTH), BF16),
            v((TOK, WIDTH), BF16), v((TOK, WIDTH), BF16), v((TOK, WIDTH), BF16),
            v((2, HALF, WIDTH), BF16),
            v((REQS, CACHE, HD), BF16), v((TOK, HD), BF16), v((TOK, HALF), F32),
            v((TOK, HD), BF16), v((TOK, HALF), F32),
            v((HALF, REQS * CACHE + HALF), F32), v((HALF, REQS * CACHE + HALF), BF16),
            v((TOK, WIDTH), BF16), v((TOK, WIDTH), BF16), v((TOK, HD), F32), v((TOK, HD), F32),
            v((HALF, WIDTH), BF16),
            v((TILES, SHARE, TILE), BF16), v((TILES, SHARE, TILE), BF16), v((TILES, SHARE, TILE), BF16),
            v((TILES, SHARE, TILE), BF16), v((TILES, SHARE, TILE), BF16), v((TILES, SHARE, TILE), BF16),
            dma((12,)), dma((15,)), dma((16,)), dma((16,)), dma((8,)), dma((8,)),
            dma((5,)), dma((5,)), dma((6,)), dma((6,)), dma((2, HEADS_HERE)), dma((2, HEADS_HERE)),
            dma((TILES, 5)), dma((TILES, 5)),
        ],
        compiler_params=pltpu.CompilerParams(
            collective_id=0, has_side_effects=True, vmem_limit_bytes=60 * 1024 * 1024),
    )(
        text_embed[0], image_embed[0], slot_source, segment_ids, prefix_lengths,
        attn_gain, qkv_weight.transpose(1, 0, 2), out_weight, cache_keys[0], cache_values[0],
    )
    hidden, keys, values, rms = pl.pallas_call(
        hand_over,
        out_shape=results,
        in_specs=[hbm, hbm, hbm, hbm],
        out_specs=(hbm, hbm, hbm, hbm),
        scratch_shapes=[dma((4,))],
        compiler_params=pltpu.CompilerParams(vmem_limit_bytes=1024 * 1024),
    )(*made)
    return hidden[None], keys[None], values[None], rms


def solution(mesh):
    return jax.shard_map(
        per_device,
        mesh=mesh,
        in_specs=(
            P("vis", None, "row"),
            P("vis", "col", "row"),
            P(),
            P("vis", None),
            P("vis", None),
            P("row"),
            P("row", None, "col"),
            P("col", "row"),
            P("vis", None, "row", "col"),
            P("vis", None, "row", "col"),
        ),
        out_specs=(
            P("vis", "col", "row"),
            P("vis", "row", "col"),
            P("vis", "row", "col"),
            P("vis", None),
        ),
        check_vma=False,
    )
```
